32 devices in a mesh: tm: 8 (over z, x), freq: 4 (over y, core).
Axes of the slice: x: 2, y: 2, z: 4, core: 2. Of those that a mesh axis runs over, the one named last changes fastest.
Arguments:
- visibilities: bfloat16 [2, 32, 2048, 4096], P(None, 'freq', 'tm'), may hold values from -6 to 6
- feed_gains: float32 [2, 32, 1024], P(None, 'freq'), may hold values from -4 to 4
- feed_pairs: int32 [4096, 2], replicated, may hold values from 0 to 1023
- m_order: int32 [8], replicated, may hold values from 0 to 7, each once
- beam_rows: bfloat16 [2, 8, 32, 64, 4096], P(None, 'tm', 'freq'), may hold values from -0.0625 to 0.0625
- kl_basis: bfloat16 [8, 32, 64, 512], P('tm', 'freq'), may hold values from -0.125 to 0.125
Outputs:
- kl_modes: float32 [2, 8, 512], P(None, 'tm', 'freq')
The draws below stay inside these ranges and needn't reach their ends.
Inputs may be any that keep to these rules, and one draw needn't show every extreme that they name: `m_order`: each value appears once.
All inputs are finite; a program needn't handle non-finite values.
Results may differ from the reference program's by a relative error of at most 0.0057.
Values may be sent and summed in bfloat16 or wider, within the bound.
No kernel may reach another device: no remote copies, remote signals or barrier semaphores. Data moves between devices by JAX's collectives and lax.ppermute only.
A program may use at most 192 MiB of HBM per device.

```python
import jax
import jax.numpy as jnp
from jax import lax

F = 32
T_SIZE = 2048
B = 4096
NFEED = 1024
K = 64
E = 512
M = 8


def touch_ends(entries, rng, smallest, largest):
    longest = entries.shape.index(max(entries.shape))
    spots = []
    for shift in (0, 1):
        where = [jax.random.randint(jax.random.fold_in(rng, axis), (), 0, length) for axis, length in enumerate(entries.shape)]
        where[longest] = (where[longest] + shift) % entries.shape[longest]
        spots.append(tuple(where))
    return entries.at[spots[0]].set(smallest).at[spots[1]].set(largest)


def levels(own_key, dims, cuts, smallest, top_value):
    gain = 1.0
    for position, shards_of in cuts:
        steps = jax.random.uniform(jax.random.fold_in(jax.random.fold_in(own_key, 6), position), (shards_of,), jnp.float32, smallest / len(cuts), top_value / len(cuts))
        gain = gain * jnp.repeat(jnp.exp(steps), dims[position] // shards_of).reshape((-1,) + (1,) * (len(dims) - 1 - position))
    return gain


def scatter_about(key, dims, scale, limit, pieces=(), kind=jnp.bfloat16):
    level = levels(key, dims, pieces, -0.22, 0.18) if pieces else 1.0
    entries = jax.random.normal(key, dims, jnp.float32) * scale * level
    return jnp.minimum(jnp.maximum(entries, -limit), limit).astype(kind)


def setup_inputs(seed: int = 0) -> dict:
    keys = jax.random.split(jax.random.key(seed), 7)
    visibilities = scatter_about(keys[0], (2, F, T_SIZE, B), 1.0, 6.0, ((1, 4), (2, 8)))
    feed_gains = scatter_about(keys[1], (2, F, NFEED), 0.8, 4.0, ((1, 4),), jnp.float32)
    feed_pairs = touch_ends(jax.random.randint(keys[2], (B, 2), 0, NFEED), jax.random.fold_in(keys[2], 1), 0, NFEED - 1).astype(jnp.int32)
    m_order = jax.random.permutation(keys[3], M).astype(jnp.int32)
    beam_rows = scatter_about(keys[4], (2, M, F, K, B), (2 * B) ** -0.5, 0.0625, ((1, 8), (2, 4)))
    kl_basis = scatter_about(keys[5], (M, F, K, E), (F * K) ** -0.5, 0.125, ((0, 8), (1, 4)))
    return dict(visibilities=visibilities, feed_gains=feed_gains, feed_pairs=feed_pairs, m_order=m_order, beam_rows=beam_rows, kl_basis=kl_basis)


def twiddle_table(m_order):
    shifted = (m_order - M // 2).astype(jnp.int32)
    times = jnp.arange(T_SIZE, dtype=jnp.int32)
    phase = shifted[:, None] * times[None, :] % T_SIZE
    angle = 2.0 * jnp.pi / T_SIZE * phase.astype(jnp.float32)
    norm = 1.0 / jnp.sqrt(jnp.float32(T_SIZE))
    cosine = jnp.cos(angle) * norm
    sine = jnp.sin(angle) * norm
    table = jnp.stack([jnp.stack([cosine, sine]), jnp.stack([-sine, cosine])])
    return table.astype(jnp.bfloat16)

def reference(visibilities, feed_gains, feed_pairs, m_order, beam_rows, kl_basis):
    table = twiddle_table(m_order).astype(jnp.float32)
    first = feed_pairs[:, 0]
    second = feed_pairs[:, 1]

    def one_channel(index):
        gains = feed_gains[:, index, :]
        gain_i = jnp.take(gains, first, axis=1)
        gain_j = jnp.take(gains, second, axis=1)
        prod_re = gain_i[0] * gain_j[0] + gain_i[1] * gain_j[1]
        prod_im = gain_i[1] * gain_j[0] - gain_i[0] * gain_j[1]
        raw = visibilities[:, index].astype(jnp.float32)
        cal_re = raw[0] * prod_re - raw[1] * prod_im
        cal_im = raw[0] * prod_im + raw[1] * prod_re
        calibrated = jnp.stack([cal_re, cal_im]).astype(jnp.bfloat16).astype(jnp.float32)
        spectrum = jnp.einsum('oimt,itb->omb', table, calibrated).astype(jnp.bfloat16).astype(jnp.float32)
        beam = beam_rows[:, :, index].astype(jnp.float32)
        tel_re = jnp.einsum('mkb,mb->mk', beam[0], spectrum[0]) - jnp.einsum('mkb,mb->mk', beam[1], spectrum[1])
        tel_im = jnp.einsum('mkb,mb->mk', beam[0], spectrum[1]) + jnp.einsum('mkb,mb->mk', beam[1], spectrum[0])
        return jnp.stack([tel_re, tel_im]).astype(jnp.bfloat16)
    telescope = lax.map(one_channel, jnp.arange(F, dtype=jnp.int32))
    telescope = telescope.astype(jnp.float32)
    basis = kl_basis.astype(jnp.float32)
    return jnp.einsum('fcmk,mfke->cme', telescope, basis)
```

```python
import functools

import jax
import jax.numpy as jnp
from jax import lax
from jax.experimental import pallas as pl
from jax.experimental.pallas import tpu as pltpu
from jax.sharding import PartitionSpec as P

LANES = 128
TILE = 512
PARTS = (5, 3)
MIB = 1 << 20
F32 = jnp.float32
BF16 = jnp.bfloat16


def relative_table(m_order, groups, local_times):
    me = lax.axis_index("tm")
    slots = m_order.shape[0]
    here = slots // groups
    high = groups // 4
    owners = jnp.arange(groups, dtype=jnp.int32)
    relative = (owners % high) * 4 + owners // high
    wanted = jnp.bitwise_xor(relative, me)[:, None] * here + jnp.arange(here, dtype=jnp.int32)[None, :]
    wanted = wanted.reshape(-1)
    held = jnp.sum(
        jnp.where(wanted[:, None] == jnp.arange(slots, dtype=jnp.int32)[None, :], m_order[None, :], 0), axis=1
    )
    length = local_times * groups
    times = me * local_times + jnp.arange(local_times, dtype=jnp.int32)
    phase = (held - slots // 2)[:, None] * times[None, :] % length
    angle = 2.0 * jnp.pi / length * phase.astype(F32)
    norm = 1.0 / jnp.sqrt(F32(length))
    cosine = jnp.cos(angle) * norm
    sine = jnp.sin(angle) * norm
    table = jnp.stack([jnp.stack([cosine, -sine], 1), jnp.stack([sine, cosine], 1)])
    return table.reshape(2, 2 * slots, local_times).astype(BF16)


def transform_kernel(first, rows, table_ref, vis_ref, *refs):
    outs, (held, sums, sems) = refs[:-3], refs[-3:]
    chans = held.shape[1]
    tiles = held.shape[3] // TILE

    def copy(tile, f):
        return pltpu.make_async_copy(
            vis_ref.at[:, f, :, pl.ds(first + tile * TILE, TILE)],
            held.at[:, f, :, pl.ds(tile * TILE, TILE)],
            sems.at[tile, f],
        )

    for tile in range(tiles):
        for f in range(chans):
            copy(tile, f).start()
    table_re = table_ref[0]
    table_im = table_ref[1]
    each = rows * chans // len(outs)
    for tile in range(tiles):
        cols = pl.ds(tile * TILE, TILE)
        for f in range(chans):
            copy(tile, f).wait()
            both = jnp.dot(table_re, held[0, f, :, cols], preferred_element_type=F32) + jnp.dot(
                table_im, held[1, f, :, cols], preferred_element_type=F32
            )
            for lane in range(0, TILE, LANES):
                sums[lane // LANES, pl.ds(f, rows, stride=chans), :] = both[:, lane : lane + LANES]
        for d, out in enumerate(outs):
            for lane in range(0, TILE, LANES):
                part = sums[lane // LANES, pl.ds(d * each, each), :]
                out[:, :, pl.ds(tile * TILE + lane, LANES)] = part.reshape(*out.shape[:2], LANES).astype(out.dtype)


def transform(table, visibilities, first, width):
    _, chans, times, _ = visibilities.shape
    rows = table.shape[1]
    shape = (rows // 8, 2 * chans, width)
    return pl.pallas_call(
        functools.partial(transform_kernel, first, rows),
        out_shape=[jax.ShapeDtypeStruct(shape, F32 if d == 0 else BF16) for d in range(4)],
        in_specs=[pl.BlockSpec(memory_space=pltpu.VMEM), pl.BlockSpec(memory_space=pl.ANY)],
        out_specs=[pl.BlockSpec(memory_space=pltpu.VMEM)] * 4,
        scratch_shapes=[
            pltpu.VMEM((2, chans, times, width), BF16),
            pltpu.VMEM((TILE // LANES, rows * chans, LANES), F32),
            pltpu.SemaphoreType.DMA((width // TILE, chans)),
        ],
        compiler_params=pltpu.CompilerParams(vmem_limit_bytes=36 * MIB),
        cost_estimate=pl.CostEstimate(
            flops=64 * rows * 2 * chans * times * width,
            bytes_accessed=4 * chans * times * width,
            transcendentals=0,
        ),
        name="transform",
    )(table, visibilities)


def gains_kernel(gains_ref, pairs_ref, out_ref):
    chans = gains_ref.shape[1]
    groups = gains_ref.shape[2] // LANES

    def step(tile, _):
        cols = pl.ds(pl.multiple_of(tile * LANES, LANES), LANES)
        picked = []
        for side in range(2):
            index = jnp.broadcast_to(pairs_ref[side : side + 1, cols], (chans, LANES))
            low = jnp.bitwise_and(index, LANES - 1)
            high = jnp.right_shift(index, 7)
            for c in range(2):
                value = jnp.zeros((chans, LANES), F32)
                for group in range(groups):
                    table = gains_ref[c, :, group * LANES : (group + 1) * LANES]
                    value = jnp.where(high == group, jnp.take_along_axis(table, low, axis=1), value)
                picked.append(value)
        i_re, i_im, j_re, j_im = picked
        out_ref[0:chans, cols] = i_re * j_re + i_im * j_im
        out_ref[chans : 2 * chans, cols] = i_im * j_re - i_re * j_im
        return 0

    lax.fori_loop(0, pairs_ref.shape[1] // LANES, step, 0)


def pair_gains(feed_gains, feed_pairs):
    chans = feed_gains.shape[1]
    count = feed_pairs.shape[0]
    return pl.pallas_call(
        gains_kernel,
        out_shape=jax.ShapeDtypeStruct((2 * chans, count), F32),
        in_specs=[pl.BlockSpec(memory_space=pltpu.VMEM)] * 2,
        out_specs=pl.BlockSpec(memory_space=pltpu.VMEM),
        cost_estimate=pl.CostEstimate(flops=4 << 20, bytes_accessed=4 << 20, transcendentals=0),
        name="pair_gains",
    )(feed_gains, feed_pairs.T)


def project_kernel(first, n_recv, *refs):
    keep, recvs = refs[0], refs[1 : 1 + n_recv]
    gains, beams, out = refs[1 + n_recv : 4 + n_recv]
    chans = beams.shape[1]
    modes = beams.shape[2]
    width = keep.shape[1]
    total = keep[...]
    for recv in recvs:
        total = total + recv[...].astype(F32)
    cols = pl.ds(first, width)
    p_re, p_im = gains[0:chans, cols], gains[chans : 2 * chans, cols]
    re, im = total[:chans], total[chans:]
    spec = jnp.concatenate([re * p_re - im * p_im, re * p_im + im * p_re]).astype(BF16)
    for f in range(chans):
        beam = jnp.concatenate([beams[0, f, :, cols], beams[1, f, :, cols]])
        both = lax.dot_general(spec, beam, (((1,), (1,)), ((), ())), preferred_element_type=F32)
        straight, crossed = both[:, :modes], both[:, modes:]
        out[f] = jnp.concatenate(
            [straight[:chans] - crossed[chans:], straight[chans:] + crossed[:chans]]
        )


def project(keep, recvs, gains, beams, first):
    _, chans, modes, _ = beams.shape
    width = keep.shape[1]
    return pl.pallas_call(
        functools.partial(project_kernel, first, len(recvs)),
        out_shape=jax.ShapeDtypeStruct((chans, 2 * chans, modes), F32),
        in_specs=[pl.BlockSpec(memory_space=pltpu.VMEM)] * (3 + len(recvs)),
        out_specs=pl.BlockSpec(memory_space=pltpu.VMEM),
        compiler_params=pltpu.CompilerParams(vmem_limit_bytes=24 * MIB),
        cost_estimate=pl.CostEstimate(
            flops=16 * 4 * chans * modes * width * chans, bytes_accessed=4 * chans * modes * width, transcendentals=0
        ),
        name="project",
    )(keep, *recvs, gains, beams)


def modes_kernel(n_tel, *refs):
    tels, (where_ref, basis, out) = refs[:n_tel], refs[n_tel:]
    chans = basis.shape[0]
    me = where_ref[0]
    row = lax.broadcasted_iota(jnp.int32, tels[0].shape[1:], 0)
    total = jnp.zeros((2 * chans, basis.shape[2]), F32)
    for f in range(chans):
        tel = functools.reduce(lambda a, b: a + b, [t[f] for t in tels])
        tel = jnp.where(jnp.bitwise_and(row, chans - 1) == f, tel, 0.0).astype(BF16)
        total = total + jnp.dot(tel, basis[f], preferred_element_type=F32)
    both = jnp.concatenate(
        [jnp.sum(total[:chans], axis=0, keepdims=True), jnp.sum(total[chans:], axis=0, keepdims=True)]
    )
    width = out.shape[2]
    for block in range(out.shape[0]):
        out[jnp.bitwise_xor(block, me)] = both[:, block * width : (block + 1) * width]


def partial_modes(tels, basis, blocks):
    where = lax.axis_index("freq").astype(jnp.int32).reshape(1)
    return pl.pallas_call(
        functools.partial(modes_kernel, len(tels)),
        out_shape=jax.ShapeDtypeStruct((blocks, 2, basis.shape[2] // blocks), F32),
        in_specs=[pl.BlockSpec(memory_space=pltpu.VMEM)] * len(tels)
        + [pl.BlockSpec(memory_space=pltpu.SMEM), pl.BlockSpec(memory_space=pltpu.VMEM)],
        out_specs=pl.BlockSpec(memory_space=pltpu.VMEM),
        name="partial_modes",
    )(*tels, where, basis)


def swap(x, axis, mask):
    return lax.ppermute(x, axis, [(i, i ^ mask) for i in range(lax.axis_size(axis))])


def reduce_slots(parts, groups):
    shift = 0
    while True:
        received = [swap(part, "tm", d << shift) for d, part in enumerate(parts) if d]
        left = groups >> (shift + (len(parts) - 1).bit_length())
        if left == 1:
            return parts[0][0], [r[0] for r in received]
        total = parts[0] + functools.reduce(lambda a, b: a + b, [r.astype(F32) for r in received])
        shift += (len(parts) - 1).bit_length()
        ways = min(4, left)
        total = total.reshape(left // ways, ways, *total.shape[1:])
        parts = [total[:, d] if d == 0 else total[:, d].astype(BF16) for d in range(ways)]


def on_device(visibilities, feed_gains, feed_pairs, m_order, beam_rows, kl_basis):
    groups = lax.axis_size("tm")
    count = visibilities.shape[3]
    table = relative_table(m_order, groups, visibilities.shape[2])
    first = 0
    spectra = []
    for share in PARTS:
        width = count // sum(PARTS) * share
        parts = transform(table, visibilities, first, width)
        spectra.append((first, reduce_slots(parts, groups)))
        first += width
    gains = pair_gains(feed_gains, feed_pairs)
    tels = [project(keep, recvs, gains, beam_rows[:, 0], start) for start, (keep, recvs) in spectra]
    held = partial_modes(tels, kl_basis[0], lax.axis_size("freq"))
    held = held.reshape(held.shape[0] // 2, 2, *held.shape[1:])
    held = held[:, 0] + swap(held[:, 1], "freq", 1)
    held = held[0] + swap(held[1], "freq", 2)
    return held[:, None, :]


def solution(mesh):
    placed = (
        P(None, "freq", "tm", None),
        P(None, "freq", None),
        P(),
        P(),
        P(None, "tm", "freq", None, None),
        P("tm", "freq", None, None),
    )
    return jax.shard_map(
        on_device, mesh=mesh, in_specs=placed, out_specs=P(None, "tm", "freq"), check_vma=False
    )
```

```python
import functools

import jax
import jax.numpy as jnp
from jax import lax
from jax.experimental import pallas as pl
from jax.experimental.pallas import tpu as pltpu
from jax.sharding import PartitionSpec as P

LANES = 128
PARTS = ((5, 2), (3, 1))
MIB = 1 << 20
F32 = jnp.float32
BF16 = jnp.bfloat16
VMEM = pl.BlockSpec(memory_space=pltpu.VMEM)
SMEM = pl.BlockSpec(memory_space=pltpu.SMEM)
HBM = pl.BlockSpec(memory_space=pltpu.HBM)


def twiddles(place, order, groups, here, local_times):
    slots = groups * here
    high = groups // 4
    me = place[0]
    length = local_times * groups
    shape = (2 * slots, local_times)
    row = lax.broadcasted_iota(jnp.int32, shape, 0)
    wanted = jnp.right_shift(row, 1)
    held = jnp.zeros(shape, jnp.int32)
    for index in range(slots):
        relative, slot = divmod(index, here)
        owner = jnp.bitwise_xor(relative % high * 4 + relative // high, me)
        held = jnp.where(wanted == index, order[owner * here + slot], held)
    times = me * local_times + lax.broadcasted_iota(jnp.int32, shape, 1)
    phase = (held - slots // 2) * times
    phase = jnp.bitwise_and(phase, length - 1) if length & (length - 1) == 0 else phase % length
    angle = 2.0 * jnp.pi / length * phase.astype(F32)
    norm = 1.0 / jnp.sqrt(F32(length))
    cosine = jnp.cos(angle) * norm
    sine = jnp.sin(angle) * norm
    real = jnp.bitwise_and(row, 1) == 0
    return jnp.where(real, cosine, -sine).astype(BF16), jnp.where(real, sine, cosine).astype(BF16)


def transform_kernel(first, tiles, groups, place, order, vis_ref, *refs):
    outs, (held, sums, order_held, order_sem, sems) = refs[:-5], refs[-5:]
    _, chans, local_times, width = held.shape
    here = order.shape[0] // groups
    rows = 2 * order.shape[0]
    tile = width // tiles

    def copy(t, f):
        return pltpu.make_async_copy(
            vis_ref.at[:, f, :, pl.ds(first + t * tile, tile)],
            held.at[:, f, :, pl.ds(t * tile, tile)],
            sems.at[t, f],
        )

    for t in range(tiles):
        for f in range(chans):
            copy(t, f).start()
    order_copy = pltpu.make_async_copy(order, order_held, order_sem)
    order_copy.start()
    order_copy.wait()
    table_re, table_im = twiddles(place, order_held, groups, here, local_times)
    each = rows * chans // len(outs)
    for t in range(tiles):
        cols = pl.ds(t * tile, tile)
        for f in range(chans):
            copy(t, f).wait()
            both = jnp.dot(table_re, held[0, f, :, cols], preferred_element_type=F32) + jnp.dot(
                table_im, held[1, f, :, cols], preferred_element_type=F32
            )
            for lane in range(0, tile, LANES):
                sums[lane // LANES, pl.ds(f, rows, stride=chans), :] = both[:, lane : lane + LANES]
        for d, out in enumerate(outs):
            for lane in range(0, tile, LANES):
                part = sums[lane // LANES, pl.ds(d * each, each), :]
                out[:, :, pl.ds(t * tile + lane, LANES)] = part.reshape(*out.shape[:2], LANES).astype(out.dtype)


def transform(place, order, visibilities, first, width, tiles, groups):
    _, chans, times, _ = visibilities.shape
    rows = 2 * order.shape[0]
    shape = (rows // 8, 2 * chans, width)
    return pl.pallas_call(
        functools.partial(transform_kernel, first, tiles, groups),
        out_shape=[jax.ShapeDtypeStruct(shape, F32 if d == 0 else BF16) for d in range(4)],
        in_specs=[SMEM, HBM, HBM],
        out_specs=[VMEM] * 4,
        scratch_shapes=[
            pltpu.VMEM((2, chans, times, width), BF16),
            pltpu.VMEM((width // tiles // LANES, rows * chans, LANES), F32),
            pltpu.SMEM(order.shape, jnp.int32),
            pltpu.SemaphoreType.DMA,
            pltpu.SemaphoreType.DMA((tiles, chans)),
        ],
        compiler_params=pltpu.CompilerParams(vmem_limit_bytes=30 * MIB),
        cost_estimate=pl.CostEstimate(
            flops=64 * rows * 2 * chans * times * width,
            bytes_accessed=4 * chans * times * width,
            transcendentals=0,
        ),
        name="transform",
    )(place, order, visibilities)


def prepare_kernel(gains_ref, pairs_ref, beams_ref, out_ref, beams_out, sem):
    copy = pltpu.make_async_copy(beams_ref.at[:, 0], beams_out, sem)
    copy.start()
    chans = gains_ref.shape[1]
    groups = gains_ref.shape[2] // LANES

    def step(tile, _):
        cols = pl.ds(pl.multiple_of(tile * LANES, LANES), LANES)
        picked = []
        for side in range(2):
            index = jnp.broadcast_to(pairs_ref[side : side + 1, cols], (chans, LANES))
            low = jnp.bitwise_and(index, LANES - 1)
            high = jnp.right_shift(index, 7)
            for c in range(2):
                value = jnp.zeros((chans, LANES), F32)
                for group in range(groups):
                    table = gains_ref[c, :, group * LANES : (group + 1) * LANES]
                    value = jnp.where(high == group, jnp.take_along_axis(table, low, axis=1), value)
                picked.append(value)
        i_re, i_im, j_re, j_im = picked
        out_ref[0:chans, cols] = i_re * j_re + i_im * j_im
        out_ref[chans : 2 * chans, cols] = i_im * j_re - i_re * j_im
        return 0

    lax.fori_loop(0, pairs_ref.shape[1] // LANES, step, 0, unroll=8)
    copy.wait()


def prepare(feed_gains, feed_pairs, beam_rows):
    chans = feed_gains.shape[1]
    count = feed_pairs.shape[0]
    beams = (beam_rows.shape[0], *beam_rows.shape[2:])
    return pl.pallas_call(
        prepare_kernel,
        out_shape=[jax.ShapeDtypeStruct((2 * chans, count), F32), jax.ShapeDtypeStruct(beams, BF16)],
        in_specs=[VMEM, VMEM, HBM],
        out_specs=[VMEM, VMEM],
        scratch_shapes=[pltpu.SemaphoreType.DMA],
        compiler_params=pltpu.CompilerParams(vmem_limit_bytes=12 * MIB),
        cost_estimate=pl.CostEstimate(flops=4 << 20, bytes_accessed=9 << 20, transcendentals=0),
        name="prepare",
    )(feed_gains, feed_pairs.T, beam_rows)


def project_kernel(first, n_recv, *refs):
    keep, recvs = refs[0], refs[1 : 1 + n_recv]
    gains, beams, out = refs[1 + n_recv : 4 + n_recv]
    for f, value in enumerate(telescope(first, keep, recvs, gains, beams)):
        out[f] = value


def telescope(first, keep, recvs, gains, beams):
    _, chans, modes, _ = beams.shape
    width = keep.shape[1]
    total = keep[...]
    for recv in recvs:
        total = total + recv[...].astype(F32)
    cols = pl.ds(first, width)
    p_re, p_im = gains[0:chans, cols], gains[chans : 2 * chans, cols]
    re, im = total[:chans], total[chans:]
    spec = jnp.concatenate([re * p_re - im * p_im, re * p_im + im * p_re]).astype(BF16)
    found = []
    for f in range(chans):
        beam = jnp.concatenate([beams[0, f, :, cols], beams[1, f, :, cols]])
        both = lax.dot_general(spec, beam, (((1,), (1,)), ((), ())), preferred_element_type=F32)
        straight, crossed = both[:, :modes], both[:, modes:]
        found.append(
            jnp.concatenate([straight[:chans] - crossed[chans:], straight[chans:] + crossed[:chans]])
        )
    return found


def project(keep, recvs, gains, beams, first):
    _, chans, modes, _ = beams.shape
    width = keep.shape[1]
    return pl.pallas_call(
        functools.partial(project_kernel, first, len(recvs)),
        out_shape=jax.ShapeDtypeStruct((chans, 2 * chans, modes), F32),
        in_specs=[VMEM] * (3 + len(recvs)),
        out_specs=VMEM,
        compiler_params=pltpu.CompilerParams(vmem_limit_bytes=8 * MIB),
        cost_estimate=pl.CostEstimate(
            flops=16 * 4 * chans * modes * width * chans, bytes_accessed=4 * chans * modes * width, transcendentals=0
        ),
        name="project",
    )(keep, *recvs, gains, beams)


def finish_kernel(first, n_recv, n_tel, place, *refs):
    keep, recvs = refs[0], refs[1 : 1 + n_recv]
    gains, beams, basis = refs[1 + n_recv : 4 + n_recv]
    tels, outs = refs[4 + n_recv : 4 + n_recv + n_tel], refs[4 + n_recv + n_tel :]
    chans = basis.shape[0]
    last = telescope(first, keep, recvs, gains, beams)
    row = lax.broadcasted_iota(jnp.int32, last[0].shape, 0)
    total = jnp.zeros((2 * chans, basis.shape[2]), F32)
    for f in range(chans):
        tel = functools.reduce(lambda a, b: a + b, [t[f] for t in tels], last[f])
        tel = jnp.where(jnp.bitwise_and(row, chans - 1) == f, tel, 0.0).astype(BF16)
        total = total + jnp.dot(tel, basis[f], preferred_element_type=F32)
    both = jnp.concatenate(
        [jnp.sum(total[:chans], axis=0, keepdims=True), jnp.sum(total[chans:], axis=0, keepdims=True)]
    )
    me = place[1]
    width = outs[0].shape[2]
    for half, out in enumerate(outs):
        for high in range(out.shape[0]):
            value = jnp.zeros((2, width), F32)
            for block in range(2 * out.shape[0]):
                part = both[:, block * width : (block + 1) * width]
                value = jnp.where(jnp.bitwise_xor(block, me) == 2 * high + half, part, value)
            out[high] = value


def finish(place, keep, recvs, gains, beams, first, tels, basis, blocks):
    shape = jax.ShapeDtypeStruct((blocks // 2, 2, basis.shape[2] // blocks), F32)
    return pl.pallas_call(
        functools.partial(finish_kernel, first, len(recvs), len(tels)),
        out_shape=[shape, shape],
        in_specs=[SMEM] + [VMEM] * (4 + len(recvs) + len(tels)),
        out_specs=[VMEM, VMEM],
        compiler_params=pltpu.CompilerParams(vmem_limit_bytes=8 * MIB),
        name="finish",
    )(place, keep, *recvs, gains, beams, basis, *tels)


def swap(x, axis, mask):
    return lax.ppermute(x, axis, [(i, i ^ mask) for i in range(lax.axis_size(axis))])


def exchange(parts, shift):
    return [swap(part, "tm", d << shift) for d, part in enumerate(parts) if d]


def combine(parts, received, left):
    total = parts[0] + functools.reduce(lambda a, b: a + b, [r.astype(F32) for r in received])
    ways = min(4, left)
    total = total.reshape(left // ways, ways, *total.shape[1:])
    return [total[:, d] if d == 0 else total[:, d].astype(BF16) for d in range(ways)]


def on_device(visibilities, feed_gains, feed_pairs, m_order, beam_rows, kl_basis):
    groups = lax.axis_size("tm")
    count = visibilities.shape[3]
    place = jnp.stack([lax.axis_index("tm"), lax.axis_index("freq")]).astype(jnp.int32)
    shares = sum(share for share, _ in PARTS)
    firsts, sent, arrived = [0], [], []
    for share, tiles in PARTS:
        width = count // shares * share
        parts = transform(place, m_order, visibilities, firsts[-1], width, tiles, groups)
        if arrived:
            parts, arrived[-1][:1] = lax.optimization_barrier((parts, arrived[-1][:1]))
        sent.append(parts)
        arrived.append(exchange(parts, 0))
        firsts.append(firsts[-1] + width)
    spectra = []
    for index, (parts, received) in enumerate(zip(sent, arrived)):
        left, shift = groups // 4, 2
        if index == len(PARTS) - 1:
            received, gains = lax.optimization_barrier((received, gains))
        while left > 1:
            parts = combine(parts, received, left)
            received = exchange(parts, shift)
            left, shift = left // len(parts), shift + (len(parts) - 1).bit_length()
        if index == 0:
            feed_gains, parts = lax.optimization_barrier((feed_gains, parts))
            gains, beams = prepare(feed_gains, feed_pairs, beam_rows)
        spectra.append((parts[0][0], [r[0] for r in received]))
    tels = [project(keep, recvs, gains, beams, first) for first, (keep, recvs) in zip(firsts, spectra[:-1])]
    keep, recvs = spectra[-1]
    held, sent = finish(place, keep, recvs, gains, beams, firsts[-2], tels, kl_basis[0], lax.axis_size("freq"))
    held = held + swap(sent, "freq", 1)
    held = held[0] + swap(held[1], "freq", 2)
    return held[:, None, :]


def solution(mesh):
    placed = (
        P(None, "freq", "tm", None),
        P(None, "freq", None),
        P(),
        P(),
        P(None, "tm", "freq", None, None),
        P("tm", "freq", None, None),
    )
    return jax.shard_map(
        on_device, mesh=mesh, in_specs=placed, out_specs=P(None, "tm", "freq"), check_vma=False
    )
```

```python
import functools

import jax
import jax.numpy as jnp
from jax import lax
from jax.experimental import pallas as pl
from jax.experimental.pallas import tpu as pltpu
from jax.sharding import PartitionSpec as P

LANES = 128
PARTS = ((11,11), (10,))
SHARES = 32
MIB = 1 << 20
F32 = jnp.float32
BF16 = jnp.bfloat16
VMEM = pl.BlockSpec(memory_space=pltpu.VMEM)
SMEM = pl.BlockSpec(memory_space=pltpu.SMEM)
HBM = pl.BlockSpec(memory_space=pltpu.HBM)


def twiddles(place, order, groups, here, local_times):
    slots = groups * here
    high = groups // 4
    me = place[0]
    length = local_times * groups
    shape = (2 * slots, local_times)
    row = lax.broadcasted_iota(jnp.int32, shape, 0)
    wanted = jnp.right_shift(row, 1)
    held = jnp.zeros(shape, jnp.int32)
    for index in range(slots):
        relative, slot = divmod(index, here)
        owner = jnp.bitwise_xor(relative % high * 4 + relative // high, me)
        held = jnp.where(wanted == index, order[owner * here + slot], held)
    times = me * local_times + lax.broadcasted_iota(jnp.int32, shape, 1)
    phase = (held - slots // 2) * times
    phase = jnp.bitwise_and(phase, length - 1) if length & (length - 1) == 0 else phase % length
    angle = 2.0 * jnp.pi / length * phase.astype(F32)
    norm = 1.0 / jnp.sqrt(F32(length))
    cosine = jnp.cos(angle) * norm
    sine = jnp.sin(angle) * norm
    real = jnp.bitwise_and(row, 1) == 0
    return jnp.where(real, cosine, -sine).astype(BF16), jnp.where(real, sine, cosine).astype(BF16)


def transform_kernel(first, ends, groups, place, order, vis_ref, *refs):
    outs, (held, sums, order_held, order_sem, sems) = refs[:-5], refs[-5:]
    _, chans, local_times, _ = held.shape
    here = order.shape[0] // groups
    rows = 2 * order.shape[0]
    tiles = list(zip((0, *ends), ends))

    def copy(t, f):
        begin, end = tiles[t]
        return pltpu.make_async_copy(
            vis_ref.at[:, f, :, pl.ds(first + begin, end - begin)],
            held.at[:, f, :, pl.ds(begin, end - begin)],
            sems.at[t, f],
        )

    for t in range(len(tiles)):
        for f in range(chans):
            copy(t, f).start()
    order_copy = pltpu.make_async_copy(order, order_held, order_sem)
    order_copy.start()
    order_copy.wait()
    table_re, table_im = twiddles(place, order_held, groups, here, local_times)
    each = rows * chans // len(outs)
    for t, (begin, end) in enumerate(tiles):
        cols = pl.ds(begin, end - begin)
        for f in range(chans):
            copy(t, f).wait()
            both = jnp.dot(table_re, held[0, f, :, cols], preferred_element_type=F32) + jnp.dot(
                table_im, held[1, f, :, cols], preferred_element_type=F32
            )
            for lane in range(0, end - begin, LANES):
                sums[lane // LANES, pl.ds(f, rows, stride=chans), :] = both[:, lane : lane + LANES]
        for d, out in enumerate(outs):
            for lane in range(0, end - begin, LANES):
                part = sums[lane // LANES, pl.ds(d * each, each), :]
                out[:, :, pl.ds(begin + lane, LANES)] = part.reshape(*out.shape[:2], LANES).astype(out.dtype)


def transform(place, order, visibilities, first, ends, groups):
    _, chans, times, _ = visibilities.shape
    rows = 2 * order.shape[0]
    width = ends[-1]
    widest = max(end - begin for begin, end in zip((0, *ends), ends))
    shape = (rows // 8, 2 * chans, width)
    return pl.pallas_call(
        functools.partial(transform_kernel, first, ends, groups),
        out_shape=[jax.ShapeDtypeStruct(shape, F32 if d == 0 else BF16) for d in range(4)],
        in_specs=[SMEM, HBM, HBM],
        out_specs=[VMEM] * 4,
        scratch_shapes=[
            pltpu.VMEM((2, chans, times, width), BF16),
            pltpu.VMEM((widest // LANES, rows * chans, LANES), F32),
            pltpu.SMEM(order.shape, jnp.int32),
            pltpu.SemaphoreType.DMA,
            pltpu.SemaphoreType.DMA((len(ends), chans)),
        ],
        compiler_params=pltpu.CompilerParams(vmem_limit_bytes=30 * MIB),
        cost_estimate=pl.CostEstimate(
            flops=64 * rows * 2 * chans * times * width,
            bytes_accessed=4 * chans * times * width,
            transcendentals=0,
        ),
        name="transform",
    )(place, order, visibilities)


def pair_gains_kernel(gains_ref, pairs_ref, out_ref):
    chans = gains_ref.shape[1]
    groups = gains_ref.shape[2] // LANES

    def step(tile, _):
        cols = pl.ds(pl.multiple_of(tile * LANES, LANES), LANES)
        picked = []
        for side in range(2):
            index = jnp.broadcast_to(pairs_ref[side : side + 1, cols], (chans, LANES))
            low = jnp.bitwise_and(index, LANES - 1)
            high = jnp.right_shift(index, 7)
            for c in range(2):
                value = jnp.zeros((chans, LANES), F32)
                for group in range(groups):
                    table = gains_ref[c, :, group * LANES : (group + 1) * LANES]
                    value = jnp.where(high == group, jnp.take_along_axis(table, low, axis=1), value)
                picked.append(value)
        i_re, i_im, j_re, j_im = picked
        out_ref[0:chans, cols] = i_re * j_re + i_im * j_im
        out_ref[chans : 2 * chans, cols] = i_im * j_re - i_re * j_im
        return 0

    lax.fori_loop(0, pairs_ref.shape[1] // LANES, step, 0, unroll=8)


def pair_gains(feed_gains, feed_pairs):
    chans = feed_gains.shape[1]
    count = feed_pairs.shape[0]
    return pl.pallas_call(
        pair_gains_kernel,
        out_shape=jax.ShapeDtypeStruct((2 * chans, count), F32),
        in_specs=[VMEM, VMEM],
        out_specs=VMEM,
        compiler_params=pltpu.CompilerParams(vmem_limit_bytes=4 * MIB),
        cost_estimate=pl.CostEstimate(flops=4 << 20, bytes_accessed=4 << 20, transcendentals=0),
        name="pair_gains",
    )(feed_gains, feed_pairs.T)


def project_kernel(first, n_recv, *refs):
    keep, recvs = refs[0], refs[1 : 1 + n_recv]
    gains, beams, out = refs[1 + n_recv : 4 + n_recv]
    for f, value in enumerate(telescope(first, keep, recvs, gains, beams)):
        out[f] = value


def telescope(first, keep, recvs, gains, beams):
    _, chans, modes, _ = beams.shape
    width = keep.shape[1]
    total = keep[...]
    for recv in recvs:
        total = total + recv[...].astype(F32)
    cols = pl.ds(first, width)
    p_re, p_im = gains[0:chans, cols], gains[chans : 2 * chans, cols]
    re, im = total[:chans], total[chans:]
    spec = jnp.concatenate([re * p_re - im * p_im, re * p_im + im * p_re]).astype(BF16)
    found = []
    for f in range(0, chans, 2):
        beam = jnp.concatenate([beams[0, f, :, cols], beams[0, f + 1, :, cols], beams[1, f, :, cols], beams[1, f + 1, :, cols]])
        both = lax.dot_general(spec, beam, (((1,), (1,)), ((), ())), preferred_element_type=F32)
        straight, crossed = both[:, : 2 * modes], both[:, 2 * modes :]
        found.append(
            jnp.concatenate([straight[:chans] - crossed[chans:], straight[chans:] + crossed[:chans]])
        )
    return found


def project(keep, recvs, gains, beams, first):
    _, chans, modes, _ = beams.shape
    width = keep.shape[1]
    return pl.pallas_call(
        functools.partial(project_kernel, first, len(recvs)),
        out_shape=jax.ShapeDtypeStruct((chans // 2, 2 * chans, 2 * modes), F32),
        in_specs=[VMEM] * (3 + len(recvs)),
        out_specs=VMEM,
        compiler_params=pltpu.CompilerParams(vmem_limit_bytes=8 * MIB),
        cost_estimate=pl.CostEstimate(
            flops=16 * 4 * chans * modes * width * chans, bytes_accessed=4 * chans * modes * width, transcendentals=0
        ),
        name="project",
    )(keep, *recvs, gains, beams)


def finish_kernel(first, n_recv, n_tel, place, *refs):
    keep, recvs = refs[0], refs[1 : 1 + n_recv]
    gains, beams, basis = refs[1 + n_recv : 4 + n_recv]
    tels, outs = refs[4 + n_recv : 4 + n_recv + n_tel], refs[4 + n_recv + n_tel :]
    chans = 2 * basis.shape[0]
    last = telescope(first, keep, recvs, gains, beams)
    shape = last[0].shape
    channel = lax.broadcasted_iota(jnp.int32, shape, 0) % chans
    second = (lax.broadcasted_iota(jnp.int32, shape, 1) >= shape[1] // 2).astype(jnp.int32)
    total = jnp.zeros((2 * chans, basis.shape[2]), F32)
    for pair, tel in enumerate(last):
        tel = functools.reduce(lambda a, b: a + b, [t[pair] for t in tels], tel)
        tel = jnp.where(channel == 2 * pair + second, tel, 0.0).astype(BF16)
        total = total + jnp.dot(tel, basis[pair], preferred_element_type=F32)
    both = jnp.concatenate(
        [jnp.sum(total[:chans], axis=0, keepdims=True), jnp.sum(total[chans:], axis=0, keepdims=True)]
    )
    me = place[1]
    width = outs[0].shape[1]
    for apart, out in enumerate(outs):
        value = jnp.zeros((2, width), F32)
        for block in range(len(outs)):
            part = both[:, block * width : (block + 1) * width]
            value = jnp.where(jnp.bitwise_xor(block, me) == apart, part, value)
        out[...] = value


def finish(place, keep, recvs, gains, beams, first, tels, basis, blocks):
    shape = jax.ShapeDtypeStruct((2, basis.shape[2] // blocks), F32)
    return pl.pallas_call(
        functools.partial(finish_kernel, first, len(recvs), len(tels)),
        out_shape=[shape] * blocks,
        in_specs=[SMEM] + [VMEM] * (4 + len(recvs) + len(tels)),
        out_specs=[VMEM] * blocks,
        compiler_params=pltpu.CompilerParams(vmem_limit_bytes=8 * MIB),
        name="finish",
    )(place, keep, *recvs, gains, beams, basis, *tels)


def swap(x, axis, mask):
    return lax.ppermute(x, axis, [(i, i ^ mask) for i in range(lax.axis_size(axis))])


def exchange(parts, shift):
    return [swap(part, "tm", d << shift) for d, part in enumerate(parts) if d]


def combine(parts, received, left):
    total = parts[0] + functools.reduce(lambda a, b: a + b, [r.astype(F32) for r in received])
    ways = min(4, left)
    total = total.reshape(left // ways, ways, *total.shape[1:])
    return [total[:, d] if d == 0 else total[:, d].astype(BF16) for d in range(ways)]


def on_device(visibilities, feed_gains, feed_pairs, m_order, beam_rows, kl_basis):
    groups = lax.axis_size("tm")
    count = visibilities.shape[3]
    place = jnp.stack([lax.axis_index("tm"), lax.axis_index("freq")]).astype(jnp.int32)
    firsts, sent, arrived = [0], [], []
    for tiles in PARTS:
        ends = tuple(count // SHARES * sum(tiles[: t + 1]) for t in range(len(tiles)))
        parts = transform(place, m_order, visibilities, firsts[-1], ends, groups)
        if arrived:
            parts, arrived[-1][:1] = lax.optimization_barrier((parts, arrived[-1][:1]))
        sent.append(parts)
        arrived.append(exchange(parts, 0))
        firsts.append(firsts[-1] + ends[-1])
    spectra = []
    beams = beam_rows[:, 0]
    for index, (parts, received) in enumerate(zip(sent, arrived)):
        left, shift = groups // 4, 2
        if index == len(PARTS) - 1:
            received, gains = lax.optimization_barrier((received, gains))
        while left > 1:
            parts = combine(parts, received, left)
            received = exchange(parts, shift)
            left, shift = left // len(parts), shift + (len(parts) - 1).bit_length()
        if index == 0:
            feed_gains, parts = lax.optimization_barrier((feed_gains, parts))
            gains = pair_gains(feed_gains, feed_pairs)
        spectra.append((parts[0][0], [r[0] for r in received]))
    tels = [project(keep, recvs, gains, beams, first) for first, (keep, recvs) in zip(firsts, spectra[:-1])]
    keep, recvs = spectra[-1]
    basis = kl_basis.reshape(kl_basis.shape[1] // 2, 2 * kl_basis.shape[2], kl_basis.shape[3])
    held, *sent = finish(place, keep, recvs, gains, beams, firsts[-2], tels, basis, lax.axis_size("freq"))
    held = functools.reduce(lambda a, b: a + b, [swap(part, "freq", d + 1) for d, part in enumerate(sent)], held)
    return held[:, None, :]


def solution(mesh):
    placed = (
        P(None, "freq", "tm", None),
        P(None, "freq", None),
        P(),
        P(),
        P(None, "tm", "freq", None, None),
        P("tm", "freq", None, None),
    )
    return jax.shard_map(
        on_device, mesh=mesh, in_specs=placed, out_specs=P(None, "tm", "freq"), check_vma=False
    )
```

```python
import functools

import jax
import jax.numpy as jnp
from jax import lax
from jax.experimental import pallas as pl
from jax.experimental.pallas import tpu as pltpu
from jax.sharding import PartitionSpec as P

LANES = 128
PARTS = ((11, 11), (10,))
SHARES = 32
MIB = 1 << 20
F32 = jnp.float32
BF16 = jnp.bfloat16
VMEM = pl.BlockSpec(memory_space=pltpu.VMEM)
SMEM = pl.BlockSpec(memory_space=pltpu.SMEM)
HBM = pl.BlockSpec(memory_space=pltpu.HBM)


def twiddles(place, groups, here, local_times):
    slots = groups * here
    high = groups // 4
    me = place[0]
    length = local_times * groups
    shape = (2 * slots, local_times)
    row = lax.broadcasted_iota(jnp.int32, shape, 0)
    wanted = jnp.right_shift(row, 1)
    held = jnp.zeros(shape, jnp.int32)
    for index in range(slots):
        relative, slot = divmod(index, here)
        owner = jnp.bitwise_xor(relative % high * 4 + relative // high, me)
        held = jnp.where(wanted == index, place[2 + owner * here + slot], held)
    times = me * local_times + lax.broadcasted_iota(jnp.int32, shape, 1)
    phase = (held - slots // 2) * times
    phase = jnp.bitwise_and(phase, length - 1) if length & (length - 1) == 0 else phase % length
    angle = 2.0 * jnp.pi / length * phase.astype(F32)
    norm = 1.0 / jnp.sqrt(F32(length))
    cosine = jnp.cos(angle) * norm
    sine = jnp.sin(angle) * norm
    real = jnp.bitwise_and(row, 1) == 0
    return jnp.where(real, cosine, -sine).astype(BF16), jnp.where(real, sine, cosine).astype(BF16)


def transform_kernel(first, ends, groups, place, vis_ref, *refs):
    outs, (held, sums, sems) = refs[:-3], refs[-3:]
    _, chans, local_times, _ = held.shape
    here = (place.shape[0] - 2) // groups
    rows = 2 * groups * here
    tiles = list(zip((0, *ends), ends))

    def copy(t, f):
        begin, end = tiles[t]
        return pltpu.make_async_copy(
            vis_ref.at[:, f, :, pl.ds(first + begin, end - begin)],
            held.at[:, f, :, pl.ds(begin, end - begin)],
            sems.at[t, f],
        )

    for t in range(len(tiles)):
        for f in range(chans):
            copy(t, f).start()
    table_re, table_im = twiddles(place, groups, here, local_times)
    each = rows * chans // len(outs)
    for t, (begin, end) in enumerate(tiles):
        cols = pl.ds(begin, end - begin)
        for f in range(chans):
            copy(t, f).wait()
            both = jnp.dot(table_re, held[0, f, :, cols], preferred_element_type=F32) + jnp.dot(
                table_im, held[1, f, :, cols], preferred_element_type=F32
            )
            for lane in range(0, end - begin, LANES):
                sums[lane // LANES, pl.ds(f, rows, stride=chans), :] = both[:, lane : lane + LANES]
        for d, out in enumerate(outs):
            for lane in range(0, end - begin, LANES):
                part = sums[lane // LANES, pl.ds(d * each, each), :]
                out[:, :, pl.ds(begin + lane, LANES)] = part.reshape(*out.shape[:2], LANES).astype(out.dtype)


def transform(place, visibilities, first, ends, groups):
    _, chans, times, _ = visibilities.shape
    rows = 2 * (place.shape[0] - 2)
    width = ends[-1]
    widest = max(end - begin for begin, end in zip((0, *ends), ends))
    shape = (rows // 8, 2 * chans, width)
    return pl.pallas_call(
        functools.partial(transform_kernel, first, ends, groups),
        out_shape=[jax.ShapeDtypeStruct(shape, F32 if d == 0 else BF16) for d in range(4)],
        in_specs=[SMEM, HBM],
        out_specs=[VMEM] * 4,
        scratch_shapes=[
            pltpu.VMEM((2, chans, times, width), BF16),
            pltpu.VMEM((widest // LANES, rows * chans, LANES), F32),
            pltpu.SemaphoreType.DMA((len(ends), chans)),
        ],
        compiler_params=pltpu.CompilerParams(vmem_limit_bytes=30 * MIB),
        cost_estimate=pl.CostEstimate(
            flops=64 * rows * 2 * chans * times * width,
            bytes_accessed=4 * chans * times * width,
            transcendentals=0,
        ),
        name="transform",
    )(place, visibilities)


def pair_gains_kernel(gains_ref, pairs_ref, out_ref):
    chans = gains_ref.shape[1]
    groups = gains_ref.shape[2] // LANES

    def step(tile, _):
        cols = pl.ds(pl.multiple_of(tile * LANES, LANES), LANES)
        picked = []
        for side in range(2):
            index = jnp.broadcast_to(pairs_ref[side : side + 1, cols], (chans, LANES))
            low = jnp.bitwise_and(index, LANES - 1)
            high = jnp.right_shift(index, 7)
            for c in range(2):
                value = jnp.zeros((chans, LANES), F32)
                for group in range(groups):
                    table = gains_ref[c, :, group * LANES : (group + 1) * LANES]
                    value = jnp.where(high == group, jnp.take_along_axis(table, low, axis=1), value)
                picked.append(value)
        i_re, i_im, j_re, j_im = picked
        out_ref[0:chans, cols] = i_re * j_re + i_im * j_im
        out_ref[chans : 2 * chans, cols] = i_im * j_re - i_re * j_im
        return 0

    lax.fori_loop(0, pairs_ref.shape[1] // LANES, step, 0, unroll=8)


def pair_gains(feed_gains, feed_pairs):
    chans = feed_gains.shape[1]
    count = feed_pairs.shape[0]
    return pl.pallas_call(
        pair_gains_kernel,
        out_shape=jax.ShapeDtypeStruct((2 * chans, count), F32),
        in_specs=[VMEM, VMEM],
        out_specs=VMEM,
        compiler_params=pltpu.CompilerParams(vmem_limit_bytes=4 * MIB),
        cost_estimate=pl.CostEstimate(flops=4 << 20, bytes_accessed=4 << 20, transcendentals=0),
        name="pair_gains",
    )(feed_gains, feed_pairs.T)


def project_kernel(first, n_recv, *refs):
    keep, recvs = refs[0], refs[1 : 1 + n_recv]
    gains, beams, out = refs[1 + n_recv : 4 + n_recv]
    for f, value in enumerate(telescope(first, keep, recvs, gains, beams)):
        out[f] = value


def telescope(first, keep, recvs, gains, beams):
    _, chans, modes, _ = beams.shape
    width = keep.shape[1]
    total = keep[...]
    for recv in recvs:
        total = total + recv[...].astype(F32)
    cols = pl.ds(first, width)
    p_re, p_im = gains[0:chans, cols], gains[chans : 2 * chans, cols]
    re, im = total[:chans], total[chans:]
    spec = jnp.concatenate([re * p_re - im * p_im, re * p_im + im * p_re]).astype(BF16)
    found = []
    for f in range(0, chans, 2):
        beam = jnp.concatenate([beams[0, f, :, cols], beams[0, f + 1, :, cols], beams[1, f, :, cols], beams[1, f + 1, :, cols]])
        both = lax.dot_general(spec, beam, (((1,), (1,)), ((), ())), preferred_element_type=F32)
        straight, crossed = both[:, : 2 * modes], both[:, 2 * modes :]
        found.append(
            jnp.concatenate([straight[:chans] - crossed[chans:], straight[chans:] + crossed[:chans]])
        )
    return found


def project(keep, recvs, gains, beams, first):
    _, chans, modes, _ = beams.shape
    width = keep.shape[1]
    return pl.pallas_call(
        functools.partial(project_kernel, first, len(recvs)),
        out_shape=jax.ShapeDtypeStruct((chans // 2, 2 * chans, 2 * modes), F32),
        in_specs=[VMEM] * (3 + len(recvs)),
        out_specs=VMEM,
        compiler_params=pltpu.CompilerParams(vmem_limit_bytes=8 * MIB),
        cost_estimate=pl.CostEstimate(
            flops=16 * 4 * chans * modes * width * chans, bytes_accessed=4 * chans * modes * width, transcendentals=0
        ),
        name="project",
    )(keep, *recvs, gains, beams)


def finish_kernel(first, n_recv, n_tel, place, *refs):
    keep, recvs = refs[0], refs[1 : 1 + n_recv]
    gains, beams, basis = refs[1 + n_recv : 4 + n_recv]
    tels, outs = refs[4 + n_recv : 4 + n_recv + n_tel], refs[4 + n_recv + n_tel :]
    chans = 2 * basis.shape[0]
    last = telescope(first, keep, recvs, gains, beams)
    shape = last[0].shape
    channel = lax.broadcasted_iota(jnp.int32, shape, 0) % chans
    second = (lax.broadcasted_iota(jnp.int32, shape, 1) >= shape[1] // 2).astype(jnp.int32)
    total = jnp.zeros((2 * chans, basis.shape[2]), F32)
    for pair, tel in enumerate(last):
        tel = functools.reduce(lambda a, b: a + b, [t[pair] for t in tels], tel)
        tel = jnp.where(channel == 2 * pair + second, tel, 0.0).astype(BF16)
        total = total + jnp.dot(tel, basis[pair], preferred_element_type=F32)
    both = jnp.concatenate(
        [jnp.sum(total[:chans], axis=0, keepdims=True), jnp.sum(total[chans:], axis=0, keepdims=True)]
    )
    me = place[1]
    width = outs[0].shape[1]
    for apart, out in enumerate(outs):
        value = jnp.zeros((2, width), F32)
        for block in range(len(outs)):
            part = both[:, block * width : (block + 1) * width]
            value = jnp.where(jnp.bitwise_xor(block, me) == apart, part, value)
        out[...] = value


def finish(place, keep, recvs, gains, beams, first, tels, basis, blocks):
    shape = jax.ShapeDtypeStruct((2, basis.shape[2] // blocks), F32)
    return pl.pallas_call(
        functools.partial(finish_kernel, first, len(recvs), len(tels)),
        out_shape=[shape] * blocks,
        in_specs=[SMEM] + [VMEM] * (4 + len(recvs) + len(tels)),
        out_specs=[VMEM] * blocks,
        compiler_params=pltpu.CompilerParams(vmem_limit_bytes=8 * MIB),
        name="finish",
    )(place, keep, *recvs, gains, beams, basis, *tels)


def swap(x, axis, mask):
    return lax.ppermute(x, axis, [(i, i ^ mask) for i in range(lax.axis_size(axis))])


def exchange(parts, shift):
    return [swap(parts[d], "tm", d << shift) for d in range(len(parts) - 1, 0, -1)]


def combine(parts, received, left):
    total = parts[0] + functools.reduce(lambda a, b: a + b, [r.astype(F32) for r in received])
    ways = min(4, left)
    total = total.reshape(left // ways, ways, *total.shape[1:])
    return [total[:, d] if d == 0 else total[:, d].astype(BF16) for d in range(ways)]


def on_device(visibilities, feed_gains, feed_pairs, m_order, beam_rows, kl_basis):
    groups = lax.axis_size("tm")
    count = visibilities.shape[3]
    place = jnp.stack([lax.axis_index("tm"), lax.axis_index("freq")]).astype(jnp.int32)
    place = jnp.concatenate([place, m_order])
    firsts, sent, arrived = [0], [], []
    for tiles in PARTS:
        ends = tuple(count // SHARES * sum(tiles[: t + 1]) for t in range(len(tiles)))
        parts = transform(place, visibilities, firsts[-1], ends, groups)
        if arrived:
            parts, arrived[-1][:1] = lax.optimization_barrier((parts, arrived[-1][:1]))
        sent.append(parts)
        arrived.append(exchange(parts, 0))
        firsts.append(firsts[-1] + ends[-1])
    spectra = []
    beams = beam_rows[:, 0]
    for index, (parts, received) in enumerate(zip(sent, arrived)):
        left, shift = groups // 4, 2
        if index == len(PARTS) - 1:
            received, gains = lax.optimization_barrier((received, gains))
        while left > 1:
            parts = combine(parts, received, left)
            received = exchange(parts, shift)
            left, shift = left // len(parts), shift + (len(parts) - 1).bit_length()
        if index == 0:
            feed_gains, parts = lax.optimization_barrier((feed_gains, parts))
            gains = pair_gains(feed_gains, feed_pairs)
        spectra.append((parts[0][0], [r[0] for r in received]))
    tels = [project(keep, recvs, gains, beams, first) for first, (keep, recvs) in zip(firsts, spectra[:-1])]
    keep, recvs = spectra[-1]
    basis = kl_basis.reshape(kl_basis.shape[1] // 2, 2 * kl_basis.shape[2], kl_basis.shape[3])
    held, *sent = finish(place, keep, recvs, gains, beams, firsts[-2], tels, basis, lax.axis_size("freq"))
    held = functools.reduce(lambda a, b: a + b, [swap(part, "freq", d + 1) for d, part in enumerate(sent)], held)
    return held[:, None, :]


def solution(mesh):
    placed = (
        P(None, "freq", "tm", None),
        P(None, "freq", None),
        P(),
        P(),
        P(None, "tm", "freq", None, None),
        P("tm", "freq", None, None),
    )
    return jax.shard_map(
        on_device, mesh=mesh, in_specs=placed, out_specs=P(None, "tm", "freq"), check_vma=False
    )
```

```python
import functools

import jax
import jax.numpy as jnp
from jax import lax
from jax.experimental import pallas as pl
from jax.experimental.pallas import tpu as pltpu
from jax.sharding import PartitionSpec as P

LANES = 128
PARTS = ((11, 11), (10,))
SHARES = 32
MIB = 1 << 20
F32 = jnp.float32
BF16 = jnp.bfloat16
VMEM = pl.BlockSpec(memory_space=pltpu.VMEM)
HBM = pl.BlockSpec(memory_space=pltpu.HBM)


def twiddles(place, order, groups, here, local_times):
    slots = groups * here
    high = groups // 4
    me = place[0]
    length = local_times * groups
    shape = (2 * slots, local_times)
    row = lax.broadcasted_iota(jnp.int32, shape, 0)
    wanted = jnp.right_shift(row, 1)
    held = jnp.zeros(shape, jnp.int32)
    for index in range(slots):
        relative, slot = divmod(index, here)
        owner = jnp.bitwise_xor(relative % high * 4 + relative // high, me)
        held = jnp.where(wanted == index, order[owner * here + slot], held)
    times = me * local_times + lax.broadcasted_iota(jnp.int32, shape, 1)
    phase = (held - slots // 2) * times
    phase = jnp.bitwise_and(phase, length - 1) if length & (length - 1) == 0 else phase % length
    angle = 2.0 * jnp.pi / length * phase.astype(F32)
    norm = 1.0 / jnp.sqrt(F32(length))
    cosine = jnp.cos(angle) * norm
    sine = jnp.sin(angle) * norm
    real = jnp.bitwise_and(row, 1) == 0
    return jnp.where(real, cosine, -sine).astype(BF16), jnp.where(real, sine, cosine).astype(BF16)


def transform_kernel(first, ends, groups, place_ref, order_ref, vis_ref, *refs):
    outs, (held, sums, place, order, place_sem, order_sem, sems) = refs[:-7], refs[-7:]
    _, chans, local_times, _ = held.shape
    here = order.shape[0] // groups
    rows = 2 * groups * here
    tiles = list(zip((0, *ends), ends))

    def copy(t, f):
        begin, end = tiles[t]
        return pltpu.make_async_copy(
            vis_ref.at[:, f, :, pl.ds(first + begin, end - begin)],
            held.at[:, f, :, pl.ds(begin, end - begin)],
            sems.at[t, f],
        )

    place_copy = pltpu.make_async_copy(place_ref, place, place_sem)
    place_copy.start()
    order_copy = pltpu.make_async_copy(order_ref, order, order_sem)
    order_copy.start()
    for t in range(len(tiles)):
        for f in range(chans):
            copy(t, f).start()
    place_copy.wait()
    order_copy.wait()
    table_re, table_im = twiddles(place, order, groups, here, local_times)
    each = rows * chans // len(outs)
    for t, (begin, end) in enumerate(tiles):
        cols = pl.ds(begin, end - begin)
        for f in range(chans):
            copy(t, f).wait()
            both = jnp.dot(table_re, held[0, f, :, cols], preferred_element_type=F32) + jnp.dot(
                table_im, held[1, f, :, cols], preferred_element_type=F32
            )
            for lane in range(0, end - begin, LANES):
                sums[lane // LANES, pl.ds(f, rows, stride=chans), :] = both[:, lane : lane + LANES]
        for d, out in enumerate(outs):
            for lane in range(0, end - begin, LANES):
                part = sums[lane // LANES, pl.ds(d * each, each), :]
                out[:, :, pl.ds(begin + lane, LANES)] = part.reshape(*out.shape[:2], LANES).astype(out.dtype)


def transform(place, order, visibilities, first, ends, groups):
    _, chans, times, _ = visibilities.shape
    rows = 2 * order.shape[0]
    width = ends[-1]
    widest = max(end - begin for begin, end in zip((0, *ends), ends))
    shape = (rows // 8, 2 * chans, width)
    return pl.pallas_call(
        functools.partial(transform_kernel, first, ends, groups),
        out_shape=[jax.ShapeDtypeStruct(shape, F32 if d == 0 else BF16) for d in range(4)],
        in_specs=[HBM, HBM, HBM],
        out_specs=[VMEM] * 4,
        scratch_shapes=[
            pltpu.VMEM((2, chans, times, width), BF16),
            pltpu.VMEM((widest // LANES, rows * chans, LANES), F32),
            pltpu.SMEM(place.shape, jnp.int32),
            pltpu.SMEM(order.shape, jnp.int32),
            pltpu.SemaphoreType.DMA,
            pltpu.SemaphoreType.DMA,
            pltpu.SemaphoreType.DMA((len(ends), chans)),
        ],
        compiler_params=pltpu.CompilerParams(vmem_limit_bytes=30 * MIB),
        cost_estimate=pl.CostEstimate(
            flops=64 * rows * 2 * chans * times * width,
            bytes_accessed=4 * chans * times * width,
            transcendentals=0,
        ),
        name="transform",
    )(place, order, visibilities)


def pair_gains_kernel(gains_ref, pairs_ref, out_ref):
    chans = gains_ref.shape[1]
    groups = gains_ref.shape[2] // LANES

    def step(tile, _):
        cols = pl.ds(pl.multiple_of(tile * LANES, LANES), LANES)
        picked = []
        for side in range(2):
            index = jnp.broadcast_to(pairs_ref[side : side + 1, cols], (chans, LANES))
            low = jnp.bitwise_and(index, LANES - 1)
            high = jnp.right_shift(index, 7)
            for c in range(2):
                value = jnp.zeros((chans, LANES), F32)
                for group in range(groups):
                    table = gains_ref[c, :, group * LANES : (group + 1) * LANES]
                    value = jnp.where(high == group, jnp.take_along_axis(table, low, axis=1), value)
                picked.append(value)
        i_re, i_im, j_re, j_im = picked
        out_ref[0:chans, cols] = i_re * j_re + i_im * j_im
        out_ref[chans : 2 * chans, cols] = i_im * j_re - i_re * j_im
        return 0

    lax.fori_loop(0, pairs_ref.shape[1] // LANES, step, 0, unroll=8)


def pair_gains(feed_gains, feed_pairs):
    chans = feed_gains.shape[1]
    count = feed_pairs.shape[0]
    return pl.pallas_call(
        pair_gains_kernel,
        out_shape=jax.ShapeDtypeStruct((2 * chans, count), F32),
        in_specs=[VMEM, VMEM],
        out_specs=VMEM,
        compiler_params=pltpu.CompilerParams(vmem_limit_bytes=4 * MIB),
        cost_estimate=pl.CostEstimate(flops=4 << 20, bytes_accessed=4 << 20, transcendentals=0),
        name="pair_gains",
    )(feed_gains, feed_pairs.T)


def project_kernel(first, n_recv, *refs):
    keep, recvs = refs[0], refs[1 : 1 + n_recv]
    gains, beams, out = refs[1 + n_recv : 4 + n_recv]
    for f, value in enumerate(telescope(first, keep, recvs, gains, beams)):
        out[f] = value


def telescope(first, keep, recvs, gains, beams):
    _, chans, modes, _ = beams.shape
    width = keep.shape[1]
    total = keep[...]
    for recv in recvs:
        total = total + recv[...].astype(F32)
    cols = pl.ds(first, width)
    p_re, p_im = gains[0:chans, cols], gains[chans : 2 * chans, cols]
    re, im = total[:chans], total[chans:]
    spec = jnp.concatenate([re * p_re - im * p_im, re * p_im + im * p_re]).astype(BF16)
    found = []
    for f in range(0, chans, 2):
        beam = jnp.concatenate([beams[0, f, :, cols], beams[0, f + 1, :, cols], beams[1, f, :, cols], beams[1, f + 1, :, cols]])
        both = lax.dot_general(spec, beam, (((1,), (1,)), ((), ())), preferred_element_type=F32)
        straight, crossed = both[:, : 2 * modes], both[:, 2 * modes :]
        found.append(
            jnp.concatenate([straight[:chans] - crossed[chans:], straight[chans:] + crossed[:chans]])
        )
    return found


def project(keep, recvs, gains, beams, first):
    _, chans, modes, _ = beams.shape
    width = keep.shape[1]
    return pl.pallas_call(
        functools.partial(project_kernel, first, len(recvs)),
        out_shape=jax.ShapeDtypeStruct((chans // 2, 2 * chans, 2 * modes), F32),
        in_specs=[VMEM] * (3 + len(recvs)),
        out_specs=VMEM,
        compiler_params=pltpu.CompilerParams(vmem_limit_bytes=8 * MIB),
        cost_estimate=pl.CostEstimate(
            flops=16 * 4 * chans * modes * width * chans, bytes_accessed=4 * chans * modes * width, transcendentals=0
        ),
        name="project",
    )(keep, *recvs, gains, beams)


def finish_kernel(first, n_recv, n_tel, place_ref, *refs):
    refs, place, place_sem = refs[:-2], refs[-2], refs[-1]
    place_copy = pltpu.make_async_copy(place_ref, place, place_sem)
    place_copy.start()
    keep, recvs = refs[0], refs[1 : 1 + n_recv]
    gains, beams, basis = refs[1 + n_recv : 4 + n_recv]
    tels, outs = refs[4 + n_recv : 4 + n_recv + n_tel], refs[4 + n_recv + n_tel :]
    chans = 2 * basis.shape[0]
    last = telescope(first, keep, recvs, gains, beams)
    shape = last[0].shape
    channel = lax.broadcasted_iota(jnp.int32, shape, 0) % chans
    second = (lax.broadcasted_iota(jnp.int32, shape, 1) >= shape[1] // 2).astype(jnp.int32)
    total = jnp.zeros((2 * chans, basis.shape[2]), F32)
    for pair, tel in enumerate(last):
        tel = functools.reduce(lambda a, b: a + b, [t[pair] for t in tels], tel)
        tel = jnp.where(channel == 2 * pair + second, tel, 0.0).astype(BF16)
        total = total + jnp.dot(tel, basis[pair], preferred_element_type=F32)
    both = jnp.concatenate(
        [jnp.sum(total[:chans], axis=0, keepdims=True), jnp.sum(total[chans:], axis=0, keepdims=True)]
    )
    place_copy.wait()
    me = place[1]
    width = outs[0].shape[1]
    for apart, out in enumerate(outs):
        value = jnp.zeros((2, width), F32)
        for block in range(len(outs)):
            part = both[:, block * width : (block + 1) * width]
            value = jnp.where(jnp.bitwise_xor(block, me) == apart, part, value)
        out[...] = value


def finish(place, keep, recvs, gains, beams, first, tels, basis, blocks):
    shape = jax.ShapeDtypeStruct((2, basis.shape[2] // blocks), F32)
    return pl.pallas_call(
        functools.partial(finish_kernel, first, len(recvs), len(tels)),
        out_shape=[shape] * blocks,
        in_specs=[HBM] + [VMEM] * (4 + len(recvs) + len(tels)),
        out_specs=[VMEM] * blocks,
        scratch_shapes=[pltpu.SMEM(place.shape, jnp.int32), pltpu.SemaphoreType.DMA],
        compiler_params=pltpu.CompilerParams(vmem_limit_bytes=8 * MIB),
        name="finish",
    )(place, keep, *recvs, gains, beams, basis, *tels)


def swap(x, axis, mask):
    return lax.ppermute(x, axis, [(i, i ^ mask) for i in range(lax.axis_size(axis))])


def exchange(parts, shift):
    return [swap(parts[d], "tm", d << shift) for d in range(len(parts) - 1, 0, -1)]


def combine(parts, received, left):
    total = parts[0] + functools.reduce(lambda a, b: a + b, [r.astype(F32) for r in received])
    ways = min(4, left)
    total = total.reshape(left // ways, ways, *total.shape[1:])
    return [total[:, d] if d == 0 else total[:, d].astype(BF16) for d in range(ways)]


def on_device(visibilities, feed_gains, feed_pairs, m_order, beam_rows, kl_basis):
    groups = lax.axis_size("tm")
    count = visibilities.shape[3]
    place = jnp.stack([lax.axis_index("tm"), lax.axis_index("freq")]).astype(jnp.int32)
    order = pltpu.with_memory_space_constraint(m_order, pltpu.HBM)
    firsts, sent, arrived = [0], [], []
    for tiles in PARTS:
        ends = tuple(count // SHARES * sum(tiles[: t + 1]) for t in range(len(tiles)))
        parts = transform(place, order, visibilities, firsts[-1], ends, groups)
        if arrived:
            parts, arrived[-1][:1] = lax.optimization_barrier((parts, arrived[-1][:1]))
        sent.append(parts)
        arrived.append(exchange(parts, 0))
        firsts.append(firsts[-1] + ends[-1])
    spectra = []
    beams = beam_rows[:, 0]
    for index, (parts, received) in enumerate(zip(sent, arrived)):
        left, shift = groups // 4, 2
        if index == len(PARTS) - 1:
            received, gains = lax.optimization_barrier((received, gains))
        while left > 1:
            parts = combine(parts, received, left)
            received = exchange(parts, shift)
            left, shift = left // len(parts), shift + (len(parts) - 1).bit_length()
        if index == 0:
            feed_gains, parts = lax.optimization_barrier((feed_gains, parts))
            gains = pair_gains(feed_gains, feed_pairs)
        spectra.append((parts[0][0], [r[0] for r in received]))
    tels = [project(keep, recvs, gains, beams, first) for first, (keep, recvs) in zip(firsts, spectra[:-1])]
    keep, recvs = spectra[-1]
    basis = kl_basis.reshape(kl_basis.shape[1] // 2, 2 * kl_basis.shape[2], kl_basis.shape[3])
    held, *sent = finish(place, keep, recvs, gains, beams, firsts[-2], tels, basis, lax.axis_size("freq"))
    held = functools.reduce(lambda a, b: a + b, [swap(part, "freq", d + 1) for d, part in enumerate(sent)], held)
    return held[:, None, :]


def solution(mesh):
    placed = (
        P(None, "freq", "tm", None),
        P(None, "freq", None),
        P(),
        P(),
        P(None, "tm", "freq", None, None),
        P("tm", "freq", None, None),
    )
    return jax.shard_map(
        on_device, mesh=mesh, in_specs=placed, out_specs=P(None, "tm", "freq"), check_vma=False
    )
```

```python
import functools

import jax
import jax.numpy as jnp
from jax import lax
from jax.experimental import pallas as pl
from jax.experimental.pallas import tpu as pltpu
from jax.sharding import PartitionSpec as P

LANES = 128
PARTS = ((11, 11), (10,))
SHARES = 32
MIB = 1 << 20
F32 = jnp.float32
BF16 = jnp.bfloat16
VMEM = pl.BlockSpec(memory_space=pltpu.VMEM)
HBM = pl.BlockSpec(memory_space=pltpu.HBM)


def twiddles(order, groups, here, local_times):
    slots = groups * here
    high = groups // 4
    me = lax.axis_index("tm")
    length = local_times * groups
    shape = (2 * slots, local_times)
    row = lax.broadcasted_iota(jnp.int32, shape, 0)
    wanted = jnp.right_shift(row, 1)
    held = jnp.zeros(shape, jnp.int32)
    for index in range(slots):
        relative, slot = divmod(index, here)
        owner = jnp.bitwise_xor(relative % high * 4 + relative // high, me)
        held = jnp.where(wanted == index, order[owner * here + slot], held)
    times = me * local_times + lax.broadcasted_iota(jnp.int32, shape, 1)
    phase = (held - slots // 2) * times
    phase = jnp.bitwise_and(phase, length - 1) if length & (length - 1) == 0 else phase % length
    angle = 2.0 * jnp.pi / length * phase.astype(F32)
    norm = 1.0 / jnp.sqrt(F32(length))
    cosine = jnp.cos(angle) * norm
    sine = jnp.sin(angle) * norm
    real = jnp.bitwise_and(row, 1) == 0
    return jnp.where(real, cosine, -sine).astype(BF16), jnp.where(real, sine, cosine).astype(BF16)


def transform_kernel(first, ends, groups, order_ref, vis_ref, *refs):
    outs, (held, sums, order, order_sem, sems) = refs[:-5], refs[-5:]
    _, chans, local_times, _ = held.shape
    here = order.shape[0] // groups
    rows = 2 * groups * here
    tiles = list(zip((0, *ends), ends))

    def copy(t, f):
        begin, end = tiles[t]
        return pltpu.make_async_copy(
            vis_ref.at[:, f, :, pl.ds(first + begin, end - begin)],
            held.at[:, f, :, pl.ds(begin, end - begin)],
            sems.at[t, f],
        )

    order_copy = pltpu.make_async_copy(order_ref, order, order_sem)
    order_copy.start()
    for t in range(len(tiles)):
        for f in range(chans):
            copy(t, f).start()
    order_copy.wait()
    table_re, table_im = twiddles(order, groups, here, local_times)
    each = rows * chans // len(outs)
    for t, (begin, end) in enumerate(tiles):
        cols = pl.ds(begin, end - begin)
        for f in range(chans):
            copy(t, f).wait()
            both = jnp.dot(table_re, held[0, f, :, cols], preferred_element_type=F32) + jnp.dot(
                table_im, held[1, f, :, cols], preferred_element_type=F32
            )
            for lane in range(0, end - begin, LANES):
                sums[lane // LANES, pl.ds(f, rows, stride=chans), :] = both[:, lane : lane + LANES]
        for d, out in enumerate(outs):
            for lane in range(0, end - begin, LANES):
                part = sums[lane // LANES, pl.ds(d * each, each), :]
                out[:, :, pl.ds(begin + lane, LANES)] = part.reshape(*out.shape[:2], LANES).astype(out.dtype)


def transform(order, visibilities, first, ends, groups):
    _, chans, times, _ = visibilities.shape
    rows = 2 * order.shape[0]
    width = ends[-1]
    widest = max(end - begin for begin, end in zip((0, *ends), ends))
    shape = (rows // 8, 2 * chans, width)
    return pl.pallas_call(
        functools.partial(transform_kernel, first, ends, groups),
        out_shape=[jax.ShapeDtypeStruct(shape, F32 if d == 0 else BF16) for d in range(4)],
        in_specs=[HBM, HBM],
        out_specs=[VMEM] * 4,
        scratch_shapes=[
            pltpu.VMEM((2, chans, times, width), BF16),
            pltpu.VMEM((widest // LANES, rows * chans, LANES), F32),
            pltpu.SMEM(order.shape, jnp.int32),
            pltpu.SemaphoreType.DMA,
            pltpu.SemaphoreType.DMA((len(ends), chans)),
        ],
        compiler_params=pltpu.CompilerParams(vmem_limit_bytes=30 * MIB),
        cost_estimate=pl.CostEstimate(
            flops=64 * rows * 2 * chans * times * width,
            bytes_accessed=4 * chans * times * width,
            transcendentals=0,
        ),
        name="transform",
    )(order, visibilities)


def pair_gains_kernel(gains_ref, pairs_ref, out_ref):
    chans = gains_ref.shape[1]
    groups = gains_ref.shape[2] // LANES

    def step(tile, _):
        cols = pl.ds(pl.multiple_of(tile * LANES, LANES), LANES)
        picked = []
        for side in range(2):
            index = jnp.broadcast_to(pairs_ref[side : side + 1, cols], (chans, LANES))
            low = jnp.bitwise_and(index, LANES - 1)
            high = jnp.right_shift(index, 7)
            for c in range(2):
                value = jnp.zeros((chans, LANES), F32)
                for group in range(groups):
                    table = gains_ref[c, :, group * LANES : (group + 1) * LANES]
                    value = jnp.where(high == group, jnp.take_along_axis(table, low, axis=1), value)
                picked.append(value)
        i_re, i_im, j_re, j_im = picked
        out_ref[0:chans, cols] = i_re * j_re + i_im * j_im
        out_ref[chans : 2 * chans, cols] = i_im * j_re - i_re * j_im
        return 0

    lax.fori_loop(0, pairs_ref.shape[1] // LANES, step, 0, unroll=8)


def pair_gains(feed_gains, feed_pairs):
    chans = feed_gains.shape[1]
    count = feed_pairs.shape[0]
    return pl.pallas_call(
        pair_gains_kernel,
        out_shape=jax.ShapeDtypeStruct((2 * chans, count), F32),
        in_specs=[VMEM, VMEM],
        out_specs=VMEM,
        compiler_params=pltpu.CompilerParams(vmem_limit_bytes=4 * MIB),
        cost_estimate=pl.CostEstimate(flops=4 << 20, bytes_accessed=4 << 20, transcendentals=0),
        name="pair_gains",
    )(feed_gains, feed_pairs.T)


def project_kernel(first, n_recv, *refs):
    keep, recvs = refs[0], refs[1 : 1 + n_recv]
    gains, beams, out = refs[1 + n_recv : 4 + n_recv]
    for f, value in enumerate(telescope(first, keep, recvs, gains, beams)):
        out[f] = value


def telescope(first, keep, recvs, gains, beams):
    _, chans, modes, _ = beams.shape
    width = keep.shape[1]
    total = keep[...]
    for recv in recvs:
        total = total + recv[...].astype(F32)
    cols = pl.ds(first, width)
    p_re, p_im = gains[0:chans, cols], gains[chans : 2 * chans, cols]
    re, im = total[:chans], total[chans:]
    spec = jnp.concatenate([re * p_re - im * p_im, re * p_im + im * p_re]).astype(BF16)
    found = []
    for f in range(0, chans, 2):
        beam = jnp.concatenate([beams[0, f, :, cols], beams[0, f + 1, :, cols], beams[1, f, :, cols], beams[1, f + 1, :, cols]])
        both = lax.dot_general(spec, beam, (((1,), (1,)), ((), ())), preferred_element_type=F32)
        straight, crossed = both[:, : 2 * modes], both[:, 2 * modes :]
        found.append(
            jnp.concatenate([straight[:chans] - crossed[chans:], straight[chans:] + crossed[:chans]])
        )
    return found


def project(keep, recvs, gains, beams, first):
    _, chans, modes, _ = beams.shape
    width = keep.shape[1]
    return pl.pallas_call(
        functools.partial(project_kernel, first, len(recvs)),
        out_shape=jax.ShapeDtypeStruct((chans // 2, 2 * chans, 2 * modes), F32),
        in_specs=[VMEM] * (3 + len(recvs)),
        out_specs=VMEM,
        compiler_params=pltpu.CompilerParams(vmem_limit_bytes=8 * MIB),
        cost_estimate=pl.CostEstimate(
            flops=16 * 4 * chans * modes * width * chans, bytes_accessed=4 * chans * modes * width, transcendentals=0
        ),
        name="project",
    )(keep, *recvs, gains, beams)


def finish_kernel(first, n_recv, n_tel, *refs):
    keep, recvs = refs[0], refs[1 : 1 + n_recv]
    gains, beams, basis = refs[1 + n_recv : 4 + n_recv]
    tels, outs = refs[4 + n_recv : 4 + n_recv + n_tel], refs[4 + n_recv + n_tel :]
    chans = 2 * basis.shape[0]
    last = telescope(first, keep, recvs, gains, beams)
    shape = last[0].shape
    channel = lax.broadcasted_iota(jnp.int32, shape, 0) % chans
    second = (lax.broadcasted_iota(jnp.int32, shape, 1) >= shape[1] // 2).astype(jnp.int32)
    total = jnp.zeros((2 * chans, basis.shape[2]), F32)
    for pair, tel in enumerate(last):
        tel = functools.reduce(lambda a, b: a + b, [t[pair] for t in tels], tel)
        tel = jnp.where(channel == 2 * pair + second, tel, 0.0).astype(BF16)
        total = total + jnp.dot(tel, basis[pair], preferred_element_type=F32)
    both = jnp.concatenate(
        [jnp.sum(total[:chans], axis=0, keepdims=True), jnp.sum(total[chans:], axis=0, keepdims=True)]
    )
    me = lax.axis_index("freq")
    width = outs[0].shape[1]
    for apart, out in enumerate(outs):
        value = jnp.zeros((2, width), F32)
        for block in range(len(outs)):
            part = both[:, block * width : (block + 1) * width]
            value = jnp.where(jnp.bitwise_xor(block, me) == apart, part, value)
        out[...] = value


def finish(keep, recvs, gains, beams, first, tels, basis, blocks):
    shape = jax.ShapeDtypeStruct((2, basis.shape[2] // blocks), F32)
    return pl.pallas_call(
        functools.partial(finish_kernel, first, len(recvs), len(tels)),
        out_shape=[shape] * blocks,
        in_specs=[VMEM] * (4 + len(recvs) + len(tels)),
        out_specs=[VMEM] * blocks,
        compiler_params=pltpu.CompilerParams(vmem_limit_bytes=8 * MIB),
        name="finish",
    )(keep, *recvs, gains, beams, basis, *tels)


def swap(x, axis, mask):
    return lax.ppermute(x, axis, [(i, i ^ mask) for i in range(lax.axis_size(axis))])


def exchange(parts, shift):
    return [swap(parts[d], "tm", d << shift) for d in range(len(parts) - 1, 0, -1)]


def combine(parts, received, left):
    total = parts[0] + functools.reduce(lambda a, b: a + b, [r.astype(F32) for r in received])
    ways = min(4, left)
    total = total.reshape(left // ways, ways, *total.shape[1:])
    return [total[:, d] if d == 0 else total[:, d].astype(BF16) for d in range(ways)]


def on_device(visibilities, feed_gains, feed_pairs, m_order, beam_rows, kl_basis):
    groups = lax.axis_size("tm")
    count = visibilities.shape[3]
    order = pltpu.with_memory_space_constraint(m_order, pltpu.HBM)
    firsts, sent, arrived = [0], [], []
    for tiles in PARTS:
        ends = tuple(count // SHARES * sum(tiles[: t + 1]) for t in range(len(tiles)))
        parts = transform(order, visibilities, firsts[-1], ends, groups)
        if arrived:
            parts, arrived[-1][:1] = lax.optimization_barrier((parts, arrived[-1][:1]))
        sent.append(parts)
        arrived.append(exchange(parts, 0))
        firsts.append(firsts[-1] + ends[-1])
    spectra = []
    beams = beam_rows[:, 0]
    for index, (parts, received) in enumerate(zip(sent, arrived)):
        left, shift = groups // 4, 2
        while left > 1:
            parts = combine(parts, received, left)
            received = exchange(parts, shift)
            left, shift = left // len(parts), shift + (len(parts) - 1).bit_length()
        if index == 0:
            feed_gains, parts = lax.optimization_barrier((feed_gains, parts))
            gains = pair_gains(feed_gains, feed_pairs)
        spectra.append((parts[0][0], [r[0] for r in received]))
    tels = [project(keep, recvs, gains, beams, first) for first, (keep, recvs) in zip(firsts, spectra[:-1])]
    keep, recvs = spectra[-1]
    basis = kl_basis.reshape(kl_basis.shape[1] // 2, 2 * kl_basis.shape[2], kl_basis.shape[3])
    held, *sent = finish(keep, recvs, gains, beams, firsts[-2], tels, basis, lax.axis_size("freq"))
    held = functools.reduce(lambda a, b: a + b, [swap(part, "freq", d + 1) for d, part in enumerate(sent)], held)
    return held[:, None, :]


def solution(mesh):
    placed = (
        P(None, "freq", "tm", None),
        P(None, "freq", None),
        P(),
        P(),
        P(None, "tm", "freq", None, None),
        P("tm", "freq", None, None),
    )
    return jax.shard_map(
        on_device, mesh=mesh, in_specs=placed, out_specs=P(None, "tm", "freq"), check_vma=False
    )
```

```python
import functools

import jax
import jax.numpy as jnp
from jax import lax
from jax.experimental import pallas as pl
from jax.experimental.pallas import tpu as pltpu
from jax.sharding import PartitionSpec as P

LANES = 128
PARTS = ((11, 11), (10,))
SHARES = 32
MIB = 1 << 20
F32 = jnp.float32
BF16 = jnp.bfloat16
VMEM = pl.BlockSpec(memory_space=pltpu.VMEM)
HBM = pl.BlockSpec(memory_space=pltpu.HBM)


def twiddles(order, groups, here, local_times):
    slots = groups * here
    high = groups // 4
    me = lax.axis_index("tm")
    length = local_times * groups
    shape = (2 * slots, local_times)
    row = lax.broadcasted_iota(jnp.int32, shape, 0)
    wanted = jnp.right_shift(row, 1)
    held = jnp.zeros(shape, jnp.int32)
    for index in range(slots):
        relative, slot = divmod(index, here)
        owner = jnp.bitwise_xor(relative % high * 4 + relative // high, me)
        held = jnp.where(wanted == index, order[owner * here + slot], held)
    times = me * local_times + lax.broadcasted_iota(jnp.int32, shape, 1)
    phase = (held - slots // 2) * times
    phase = jnp.bitwise_and(phase, length - 1) if length & (length - 1) == 0 else phase % length
    angle = 2.0 * jnp.pi / length * phase.astype(F32)
    norm = 1.0 / jnp.sqrt(F32(length))
    cosine = jnp.cos(angle) * norm
    sine = jnp.sin(angle) * norm
    real = jnp.bitwise_and(row, 1) == 0
    return jnp.where(real, cosine, -sine).astype(BF16), jnp.where(real, sine, cosine).astype(BF16)


def transform_kernel(first, ends, groups, order_ref, vis_ref, *refs):
    outs, (held, sums, order, order_sem, sems) = refs[:-5], refs[-5:]
    _, chans, local_times, _ = held.shape
    here = order.shape[0] // groups
    rows = 2 * groups * here
    tiles = list(zip((0, *ends), ends))

    def copy(t, f):
        begin, end = tiles[t]
        return pltpu.make_async_copy(
            vis_ref.at[:, f, :, pl.ds(first + begin, end - begin)],
            held.at[:, f, :, pl.ds(begin, end - begin)],
            sems.at[t, f],
        )

    order_copy = pltpu.make_async_copy(order_ref, order, order_sem)
    order_copy.start()
    for t in range(len(tiles)):
        for f in range(chans):
            copy(t, f).start()
    order_copy.wait()
    table_re, table_im = twiddles(order, groups, here, local_times)
    each = rows * chans // len(outs)
    for t, (begin, end) in enumerate(tiles):
        cols = pl.ds(begin, end - begin)
        for f in range(chans):
            copy(t, f).wait()
            both = jnp.dot(table_re, held[0, f, :, cols], preferred_element_type=F32) + jnp.dot(
                table_im, held[1, f, :, cols], preferred_element_type=F32
            )
            for lane in range(0, end - begin, LANES):
                sums[lane // LANES, pl.ds(f, rows, stride=chans), :] = both[:, lane : lane + LANES]
        for d, out in enumerate(outs):
            for lane in range(0, end - begin, LANES):
                part = sums[lane // LANES, pl.ds(d * each, each), :]
                out[:, :, pl.ds(begin + lane, LANES)] = part.reshape(*out.shape[:2], LANES).astype(out.dtype)


def transform(order, visibilities, first, ends, groups):
    _, chans, times, _ = visibilities.shape
    rows = 2 * order.shape[0]
    width = ends[-1]
    widest = max(end - begin for begin, end in zip((0, *ends), ends))
    shape = (rows // 8, 2 * chans, width)
    return pl.pallas_call(
        functools.partial(transform_kernel, first, ends, groups),
        out_shape=[jax.ShapeDtypeStruct(shape, F32 if d == 0 else BF16) for d in range(4)],
        in_specs=[HBM, HBM],
        out_specs=[VMEM] * 4,
        scratch_shapes=[
            pltpu.VMEM((2, chans, times, width), BF16),
            pltpu.VMEM((widest // LANES, rows * chans, LANES), F32),
            pltpu.SMEM(order.shape, jnp.int32),
            pltpu.SemaphoreType.DMA,
            pltpu.SemaphoreType.DMA((len(ends), chans)),
        ],
        compiler_params=pltpu.CompilerParams(vmem_limit_bytes=30 * MIB),
        cost_estimate=pl.CostEstimate(
            flops=64 * rows * 2 * chans * times * width,
            bytes_accessed=4 * chans * times * width,
            transcendentals=0,
        ),
        name="transform",
    )(order, visibilities)


def pair_gains_kernel(gains_ref, pairs_ref, out_ref):
    chans = gains_ref.shape[1]
    groups = gains_ref.shape[2] // LANES

    def step(tile, _):
        cols = pl.ds(pl.multiple_of(tile * LANES, LANES), LANES)
        picked = []
        for side in range(2):
            index = jnp.broadcast_to(pairs_ref[side : side + 1, cols], (chans, LANES))
            low = jnp.bitwise_and(index, LANES - 1)
            high = jnp.right_shift(index, 7)
            for c in range(2):
                value = jnp.zeros((chans, LANES), F32)
                for group in range(groups):
                    table = gains_ref[c, :, group * LANES : (group + 1) * LANES]
                    value = jnp.where(high == group, jnp.take_along_axis(table, low, axis=1), value)
                picked.append(value)
        i_re, i_im, j_re, j_im = picked
        out_ref[0:chans, cols] = i_re * j_re + i_im * j_im
        out_ref[chans : 2 * chans, cols] = i_im * j_re - i_re * j_im
        return 0

    lax.fori_loop(0, pairs_ref.shape[1] // LANES, step, 0, unroll=8)


def pair_gains(feed_gains, feed_pairs):
    chans = feed_gains.shape[1]
    count = feed_pairs.shape[0]
    return pl.pallas_call(
        pair_gains_kernel,
        out_shape=jax.ShapeDtypeStruct((2 * chans, count), F32),
        in_specs=[VMEM, VMEM],
        out_specs=VMEM,
        compiler_params=pltpu.CompilerParams(vmem_limit_bytes=4 * MIB),
        cost_estimate=pl.CostEstimate(flops=4 << 20, bytes_accessed=4 << 20, transcendentals=0),
        name="pair_gains",
    )(feed_gains, feed_pairs.T)


def project_kernel(first, n_recv, *refs):
    keep, recvs = refs[0], refs[1 : 1 + n_recv]
    gains, beams, out = refs[1 + n_recv : 4 + n_recv]
    for f, value in enumerate(telescope(first, keep, recvs, gains, beams)):
        out[f] = value


def telescope(first, keep, recvs, gains, beams):
    _, chans, modes, _ = beams.shape
    width = keep.shape[1]
    total = keep[...]
    for recv in recvs:
        total = total + recv[...].astype(F32)
    cols = pl.ds(first, width)
    p_re, p_im = gains[0:chans, cols], gains[chans : 2 * chans, cols]
    re, im = total[:chans], total[chans:]
    spec = jnp.concatenate([re * p_re - im * p_im, re * p_im + im * p_re]).astype(BF16)
    found = []
    for f in range(0, chans, 2):
        beam = jnp.concatenate([beams[0, f, :, cols], beams[0, f + 1, :, cols], beams[1, f, :, cols], beams[1, f + 1, :, cols]])
        both = lax.dot_general(spec, beam, (((1,), (1,)), ((), ())), preferred_element_type=F32)
        straight, crossed = both[:, : 2 * modes], both[:, 2 * modes :]
        found.append(
            jnp.concatenate([straight[:chans] - crossed[chans:], straight[chans:] + crossed[:chans]])
        )
    return found


def project(keep, recvs, gains, beams, first):
    _, chans, modes, _ = beams.shape
    width = keep.shape[1]
    return pl.pallas_call(
        functools.partial(project_kernel, first, len(recvs)),
        out_shape=jax.ShapeDtypeStruct((chans // 2, 2 * chans, 2 * modes), F32),
        in_specs=[VMEM] * (3 + len(recvs)),
        out_specs=VMEM,
        compiler_params=pltpu.CompilerParams(vmem_limit_bytes=8 * MIB),
        cost_estimate=pl.CostEstimate(
            flops=16 * 4 * chans * modes * width * chans, bytes_accessed=4 * chans * modes * width, transcendentals=0
        ),
        name="project",
    )(keep, *recvs, gains, beams)


def finish_kernel(first, n_recv, n_tel, *refs):
    keep, recvs = refs[0], refs[1 : 1 + n_recv]
    gains, beams, basis = refs[1 + n_recv : 4 + n_recv]
    tels, outs = refs[4 + n_recv : 4 + n_recv + n_tel], refs[4 + n_recv + n_tel :]
    chans = 2 * basis.shape[0]
    last = telescope(first, keep, recvs, gains, beams)
    shape = last[0].shape
    channel = lax.broadcasted_iota(jnp.int32, shape, 0) % chans
    second = (lax.broadcasted_iota(jnp.int32, shape, 1) >= shape[1] // 2).astype(jnp.int32)
    total = jnp.zeros((2 * chans, basis.shape[2]), F32)
    for pair, tel in enumerate(last):
        tel = functools.reduce(lambda a, b: a + b, [t[pair] for t in tels], tel)
        tel = jnp.where(channel == 2 * pair + second, tel, 0.0).astype(BF16)
        total = total + jnp.dot(tel, basis[pair], preferred_element_type=F32)
    both = jnp.concatenate(
        [jnp.sum(total[:chans], axis=0, keepdims=True), jnp.sum(total[chans:], axis=0, keepdims=True)]
    )
    me = lax.axis_index("freq")
    width = outs[0].shape[1]
    for apart, out in enumerate(outs):
        value = jnp.zeros((2, width), F32)
        for block in range(len(outs)):
            part = both[:, block * width : (block + 1) * width]
            value = jnp.where(jnp.bitwise_xor(block, me) == apart, part, value)
        out[...] = value


def finish(keep, recvs, gains, beams, first, tels, basis, blocks):
    shape = jax.ShapeDtypeStruct((2, basis.shape[2] // blocks), F32)
    return pl.pallas_call(
        functools.partial(finish_kernel, first, len(recvs), len(tels)),
        out_shape=[shape] * blocks,
        in_specs=[VMEM] * (4 + len(recvs) + len(tels)),
        out_specs=[VMEM] * blocks,
        compiler_params=pltpu.CompilerParams(vmem_limit_bytes=8 * MIB),
        name="finish",
    )(keep, *recvs, gains, beams, basis, *tels)


def swap(x, axis, mask):
    return lax.ppermute(x, axis, [(i, i ^ mask) for i in range(lax.axis_size(axis))])


def exchange(parts, shift):
    return [swap(parts[d], "tm", d << shift) for d in range(len(parts) - 1, 0, -1)]


def combine(parts, received, left):
    total = parts[0] + functools.reduce(lambda a, b: a + b, [r.astype(F32) for r in received])
    ways = min(4, left)
    total = total.reshape(left // ways, ways, *total.shape[1:])
    return [total[:, d] if d == 0 else total[:, d].astype(BF16) for d in range(ways)]


def on_device(visibilities, feed_gains, feed_pairs, m_order, beam_rows, kl_basis):
    groups = lax.axis_size("tm")
    count = visibilities.shape[3]
    order = pltpu.with_memory_space_constraint(m_order, pltpu.HBM)
    firsts, sent, arrived = [0], [], []
    for tiles in PARTS:
        ends = tuple(count // SHARES * sum(tiles[: t + 1]) for t in range(len(tiles)))
        parts = transform(order, visibilities, firsts[-1], ends, groups)
        if arrived:
            parts, arrived[-1][:1] = lax.optimization_barrier((parts, arrived[-1][:1]))
        sent.append(parts)
        arrived.append(exchange(parts, 0))
        firsts.append(firsts[-1] + ends[-1])
    spectra = []
    beams = beam_rows[:, 0]
    for index, (parts, received) in enumerate(zip(sent, arrived)):
        left, shift = groups // 4, 2
        while left > 1:
            parts = combine(parts, received, left)
            received = exchange(parts, shift)
            left, shift = left // len(parts), shift + (len(parts) - 1).bit_length()
        if index == 0:
            feed_gains, parts = lax.optimization_barrier((feed_gains, parts))
            gains = pair_gains(feed_gains, feed_pairs)
        spectra.append((parts[0][0], [r[0] for r in received]))
    tels = [project(keep, recvs, gains, beams, first) for first, (keep, recvs) in zip(firsts, spectra[:-1])]
    keep, recvs = spectra[-1]
    basis = kl_basis.reshape(kl_basis.shape[1] // 2, 2 * kl_basis.shape[2], kl_basis.shape[3])
    held, *sent = finish(keep, recvs, gains, beams, firsts[-2], tels, basis, lax.axis_size("freq"))
    held = functools.reduce(lambda a, b: a + b, [swap(sent[d - 1], "freq", d) for d in range(len(sent), 0, -1)], held)
    return held[:, None, :]


def solution(mesh):
    placed = (
        P(None, "freq", "tm", None),
        P(None, "freq", None),
        P(),
        P(),
        P(None, "tm", "freq", None, None),
        P("tm", "freq", None, None),
    )
    return jax.shard_map(
        on_device, mesh=mesh, in_specs=placed, out_specs=P(None, "tm", "freq"), check_vma=False
    )
```

```python
import functools

import jax
import jax.numpy as jnp
from jax import lax
from jax.experimental import pallas as pl
from jax.experimental.pallas import tpu as pltpu
from jax.sharding import PartitionSpec as P

LANES = 128
PARTS = ((11, 11), (10,))
SHARES = 32
MIB = 1 << 20
F32 = jnp.float32
BF16 = jnp.bfloat16
VMEM = pl.BlockSpec(memory_space=pltpu.VMEM)
HBM = pl.BlockSpec(memory_space=pltpu.HBM)


def twiddles(order, groups, here, local_times):
    slots = groups * here
    high = groups // 4
    me = lax.axis_index("tm")
    length = local_times * groups
    shape = (2 * slots, local_times)
    row = lax.broadcasted_iota(jnp.int32, shape, 0)
    wanted = jnp.right_shift(row, 1)
    held = jnp.zeros(shape, jnp.int32)
    for index in range(slots):
        relative, slot = divmod(index, here)
        owner = jnp.bitwise_xor(relative % high * 4 + relative // high, me)
        held = jnp.where(wanted == index, order[owner * here + slot], held)
    times = me * local_times + lax.broadcasted_iota(jnp.int32, shape, 1)
    phase = (held - slots // 2) * times
    phase = jnp.bitwise_and(phase, length - 1) if length & (length - 1) == 0 else phase % length
    angle = 2.0 * jnp.pi / length * phase.astype(F32)
    norm = 1.0 / jnp.sqrt(F32(length))
    cosine = jnp.cos(angle) * norm
    sine = jnp.sin(angle) * norm
    real = jnp.bitwise_and(row, 1) == 0
    return jnp.where(real, cosine, -sine).astype(BF16), jnp.where(real, sine, cosine).astype(BF16)


def transform_kernel(first, ends, groups, order_ref, vis_ref, *refs):
    outs, (held, sums, order, order_sem, sems) = refs[:-5], refs[-5:]
    _, chans, local_times, _ = held.shape
    here = order.shape[0] // groups
    rows = 2 * groups * here
    tiles = list(zip((0, *ends), ends))

    def copy(t, f):
        begin, end = tiles[t]
        return pltpu.make_async_copy(
            vis_ref.at[:, f, :, pl.ds(first + begin, end - begin)],
            held.at[:, f, :, pl.ds(begin, end - begin)],
            sems.at[t, f],
        )

    order_copy = pltpu.make_async_copy(order_ref, order, order_sem)
    order_copy.start()
    for t in range(len(tiles)):
        for f in range(chans):
            copy(t, f).start()
    order_copy.wait()
    table_re, table_im = twiddles(order, groups, here, local_times)
    each = rows * chans // len(outs)
    for t, (begin, end) in enumerate(tiles):
        cols = pl.ds(begin, end - begin)
        for f in range(chans):
            copy(t, f).wait()
            both = jnp.dot(table_re, held[0, f, :, cols], preferred_element_type=F32) + jnp.dot(
                table_im, held[1, f, :, cols], preferred_element_type=F32
            )
            for lane in range(0, end - begin, LANES):
                sums[lane // LANES, pl.ds(f, rows, stride=chans), :] = both[:, lane : lane + LANES]
        for d, out in enumerate(outs):
            for lane in range(0, end - begin, LANES):
                part = sums[lane // LANES, pl.ds(d * each, each), :]
                out[:, :, pl.ds(begin + lane, LANES)] = part.reshape(*out.shape[:2], LANES).astype(out.dtype)


def transform(order, visibilities, first, ends, groups):
    _, chans, times, _ = visibilities.shape
    rows = 2 * order.shape[0]
    width = ends[-1]
    widest = max(end - begin for begin, end in zip((0, *ends), ends))
    shape = (rows // 8, 2 * chans, width)
    return pl.pallas_call(
        functools.partial(transform_kernel, first, ends, groups),
        out_shape=[jax.ShapeDtypeStruct(shape, F32 if d == 0 else BF16) for d in range(4)],
        in_specs=[HBM, HBM],
        out_specs=[VMEM] * 4,
        scratch_shapes=[
            pltpu.VMEM((2, chans, times, width), BF16),
            pltpu.VMEM((widest // LANES, rows * chans, LANES), F32),
            pltpu.SMEM(order.shape, jnp.int32),
            pltpu.SemaphoreType.DMA,
            pltpu.SemaphoreType.DMA((len(ends), chans)),
        ],
        compiler_params=pltpu.CompilerParams(vmem_limit_bytes=30 * MIB),
        cost_estimate=pl.CostEstimate(
            flops=64 * rows * 2 * chans * times * width,
            bytes_accessed=4 * chans * times * width,
            transcendentals=0,
        ),
        name="transform",
    )(order, visibilities)


def pair_gains_kernel(gains_ref, pairs_ref, out_ref):
    chans = gains_ref.shape[1]
    groups = gains_ref.shape[2] // LANES

    def step(tile, _):
        cols = pl.ds(pl.multiple_of(tile * LANES, LANES), LANES)
        picked = []
        for side in range(2):
            index = jnp.broadcast_to(pairs_ref[side : side + 1, cols], (chans, LANES))
            low = jnp.bitwise_and(index, LANES - 1)
            high = jnp.right_shift(index, 7)
            for c in range(2):
                value = jnp.zeros((chans, LANES), F32)
                for group in range(groups):
                    table = gains_ref[c, :, group * LANES : (group + 1) * LANES]
                    value = jnp.where(high == group, jnp.take_along_axis(table, low, axis=1), value)
                picked.append(value)
        i_re, i_im, j_re, j_im = picked
        out_ref[0:chans, cols] = i_re * j_re + i_im * j_im
        out_ref[chans : 2 * chans, cols] = i_im * j_re - i_re * j_im
        return 0

    lax.fori_loop(0, pairs_ref.shape[1] // LANES, step, 0, unroll=16)


def pair_gains(feed_gains, feed_pairs):
    chans = feed_gains.shape[1]
    count = feed_pairs.shape[0]
    return pl.pallas_call(
        pair_gains_kernel,
        out_shape=jax.ShapeDtypeStruct((2 * chans, count), F32),
        in_specs=[VMEM, VMEM],
        out_specs=VMEM,
        compiler_params=pltpu.CompilerParams(vmem_limit_bytes=4 * MIB),
        cost_estimate=pl.CostEstimate(flops=4 << 20, bytes_accessed=4 << 20, transcendentals=0),
        name="pair_gains",
    )(feed_gains, feed_pairs.T)


def project_kernel(first, n_recv, *refs):
    keep, recvs = refs[0], refs[1 : 1 + n_recv]
    gains, beams, out = refs[1 + n_recv : 4 + n_recv]
    for f, value in enumerate(telescope(first, keep, recvs, gains, beams)):
        out[f] = value


def telescope(first, keep, recvs, gains, beams):
    _, chans, modes, _ = beams.shape
    width = keep.shape[1]
    total = keep[...]
    for recv in recvs:
        total = total + recv[...].astype(F32)
    cols = pl.ds(first, width)
    p_re, p_im = gains[0:chans, cols], gains[chans : 2 * chans, cols]
    re, im = total[:chans], total[chans:]
    spec = jnp.concatenate([re * p_re - im * p_im, re * p_im + im * p_re]).astype(BF16)
    found = []
    for f in range(0, chans, 2):
        beam = jnp.concatenate([beams[0, f, :, cols], beams[0, f + 1, :, cols], beams[1, f, :, cols], beams[1, f + 1, :, cols]])
        both = lax.dot_general(spec, beam, (((1,), (1,)), ((), ())), preferred_element_type=F32)
        straight, crossed = both[:, : 2 * modes], both[:, 2 * modes :]
        found.append(
            jnp.concatenate([straight[:chans] - crossed[chans:], straight[chans:] + crossed[:chans]])
        )
    return found


def project(keep, recvs, gains, beams, first):
    _, chans, modes, _ = beams.shape
    width = keep.shape[1]
    return pl.pallas_call(
        functools.partial(project_kernel, first, len(recvs)),
        out_shape=jax.ShapeDtypeStruct((chans // 2, 2 * chans, 2 * modes), F32),
        in_specs=[VMEM] * (3 + len(recvs)),
        out_specs=VMEM,
        compiler_params=pltpu.CompilerParams(vmem_limit_bytes=8 * MIB),
        cost_estimate=pl.CostEstimate(
            flops=16 * 4 * chans * modes * width * chans, bytes_accessed=4 * chans * modes * width, transcendentals=0
        ),
        name="project",
    )(keep, *recvs, gains, beams)


def finish_kernel(first, n_recv, n_tel, *refs):
    keep, recvs = refs[0], refs[1 : 1 + n_recv]
    gains, beams, basis = refs[1 + n_recv : 4 + n_recv]
    tels, outs = refs[4 + n_recv : 4 + n_recv + n_tel], refs[4 + n_recv + n_tel :]
    chans = 2 * basis.shape[0]
    last = telescope(first, keep, recvs, gains, beams)
    shape = last[0].shape
    channel = lax.broadcasted_iota(jnp.int32, shape, 0) % chans
    second = (lax.broadcasted_iota(jnp.int32, shape, 1) >= shape[1] // 2).astype(jnp.int32)
    total = jnp.zeros((2 * chans, basis.shape[2]), F32)
    for pair, tel in enumerate(last):
        tel = functools.reduce(lambda a, b: a + b, [t[pair] for t in tels], tel)
        tel = jnp.where(channel == 2 * pair + second, tel, 0.0).astype(BF16)
        total = total + jnp.dot(tel, basis[pair], preferred_element_type=F32)
    both = jnp.concatenate(
        [jnp.sum(total[:chans], axis=0, keepdims=True), jnp.sum(total[chans:], axis=0, keepdims=True)]
    )
    me = lax.axis_index("freq")
    width = outs[0].shape[1]
    for apart, out in enumerate(outs):
        value = jnp.zeros((2, width), F32)
        for block in range(len(outs)):
            part = both[:, block * width : (block + 1) * width]
            value = jnp.where(jnp.bitwise_xor(block, me) == apart, part, value)
        out[...] = value


def finish(keep, recvs, gains, beams, first, tels, basis, blocks):
    shape = jax.ShapeDtypeStruct((2, basis.shape[2] // blocks), F32)
    return pl.pallas_call(
        functools.partial(finish_kernel, first, len(recvs), len(tels)),
        out_shape=[shape] * blocks,
        in_specs=[VMEM] * (4 + len(recvs) + len(tels)),
        out_specs=[VMEM] * blocks,
        compiler_params=pltpu.CompilerParams(vmem_limit_bytes=8 * MIB),
        name="finish",
    )(keep, *recvs, gains, beams, basis, *tels)


def swap(x, axis, mask):
    return lax.ppermute(x, axis, [(i, i ^ mask) for i in range(lax.axis_size(axis))])


def exchange(parts, shift):
    return [swap(parts[d], "tm", d << shift) for d in range(len(parts) - 1, 0, -1)]


def combine(parts, received, left):
    total = parts[0] + functools.reduce(lambda a, b: a + b, [r.astype(F32) for r in received])
    ways = min(4, left)
    total = total.reshape(left // ways, ways, *total.shape[1:])
    return [total[:, d] if d == 0 else total[:, d].astype(BF16) for d in range(ways)]


def on_device(visibilities, feed_gains, feed_pairs, m_order, beam_rows, kl_basis):
    groups = lax.axis_size("tm")
    count = visibilities.shape[3]
    order = pltpu.with_memory_space_constraint(m_order, pltpu.HBM)
    firsts, sent, arrived = [0], [], []
    for tiles in PARTS:
        ends = tuple(count // SHARES * sum(tiles[: t + 1]) for t in range(len(tiles)))
        parts = transform(order, visibilities, firsts[-1], ends, groups)
        if arrived:
            parts, arrived[-1][:1] = lax.optimization_barrier((parts, arrived[-1][:1]))
        sent.append(parts)
        arrived.append(exchange(parts, 0))
        firsts.append(firsts[-1] + ends[-1])
    spectra = []
    beams = beam_rows[:, 0]
    for index, (parts, received) in enumerate(zip(sent, arrived)):
        left, shift = groups // 4, 2
        while left > 1:
            parts = combine(parts, received, left)
            received = exchange(parts, shift)
            left, shift = left // len(parts), shift + (len(parts) - 1).bit_length()
        if index == 0:
            feed_gains, parts = lax.optimization_barrier((feed_gains, parts))
            gains = pair_gains(feed_gains, feed_pairs)
        spectra.append((parts[0][0], [r[0] for r in received]))
    tels = [project(keep, recvs, gains, beams, first) for first, (keep, recvs) in zip(firsts, spectra[:-1])]
    keep, recvs = spectra[-1]
    basis = kl_basis.reshape(kl_basis.shape[1] // 2, 2 * kl_basis.shape[2], kl_basis.shape[3])
    held, *sent = finish(keep, recvs, gains, beams, firsts[-2], tels, basis, lax.axis_size("freq"))
    held = functools.reduce(lambda a, b: a + b, [swap(sent[d - 1], "freq", d) for d in range(len(sent), 0, -1)], held)
    return held[:, None, :]


def solution(mesh):
    placed = (
        P(None, "freq", "tm", None),
        P(None, "freq", None),
        P(),
        P(),
        P(None, "tm", "freq", None, None),
        P("tm", "freq", None, None),
    )
    return jax.shard_map(
        on_device, mesh=mesh, in_specs=placed, out_specs=P(None, "tm", "freq"), check_vma=False
    )
```
